256 devices in a mesh: tm: 16 (over y, x), row: 2 (over core), col: 8 (over z).
Axes of the slice: x: 4, y: 4, z: 8, core: 2. Of those that a mesh axis runs over, the one named last changes fastest.
Arguments:
- latents: bfloat16 [64, 8, 256, 384], P('tm', 'row', 'col'), may hold values from -6 to 6
- norm_gain: float32 [384], replicated, may hold values from 0.1 to 1.9
- conv_weight: bfloat16 [3, 3, 3, 384, 384], replicated, may hold values from -0.0625 to 0.0625
- conv_bias: float32 [384], replicated, may hold values from -3 to 3
- time_weight: bfloat16 [3, 384, 768], replicated, may hold values from -0.1875 to 0.1875
- time_bias: float32 [768], replicated, may hold values from -3 to 3
- spatial_weight: bfloat16 [3, 3, 384, 192], replicated, may hold values from -0.109375 to 0.109375
- spatial_bias: float32 [192], replicated, may hold values from -3 to 3
Outputs:
- decoded: bfloat16 [128, 16, 512, 192], P('tm', 'row', 'col')
The draws below stay inside these ranges and needn't reach their ends.
All inputs are finite; a program needn't handle non-finite values.
Results may differ from the reference program's by a relative error of at most 0.01.
Values may be sent and summed in bfloat16 or wider, within the bound.
No kernel may reach another device: no remote copies, remote signals or barrier semaphores. Data moves between devices by JAX's collectives and lax.ppermute only.
A program may use at most 128 MiB of HBM per device.

```python
import jax
import jax.numpy as jnp
from jax import lax

C = 384
OUTC = 192
NT = 64
NR = 8
NC = 256


def level_of(own_key, dims, shards, least, top_value):
    def one(position, shards_of):
        draws = jax.random.uniform(jax.random.fold_in(jax.random.fold_in(own_key, 6), position), (shards_of,), jnp.float32, least / len(shards), top_value / len(shards))
        return jnp.repeat(jnp.exp(draws), dims[position] // shards_of).reshape((-1,) + (1,) * (len(dims) - position - 1))

    level = one(*shards[0])
    for cut in shards[1:]:
        level = level * one(*cut)
    return level


def gaussian(key, extent, scale, bound, split=(), kind=jnp.bfloat16):
    level = level_of(key, extent, split, -0.22, 0.18) if split else 1.0
    values = jax.random.normal(key, extent, jnp.float32) * scale * level
    return jnp.minimum(jnp.maximum(values, -bound), bound).astype(kind)


def setup_inputs(seed: int = 0) -> dict:
    key_of = jax.random.split(jax.random.key(seed), 9)
    latents = gaussian(key_of[0], (NT, NR, NC, C), 1.0, 6.0, ((0, 16), (1, 2), (2, 8)))
    norm_gain = jnp.clip(1.0 + 0.18 * jax.random.normal(key_of[1], (C,), jnp.float32), 0.1, 1.9)
    conv_weight = gaussian(key_of[2], (3, 3, 3, C, C), (27 * C) ** -0.5, 0.0625)
    conv_bias = gaussian(key_of[3], (C,), 0.5, 3.0, (), jnp.float32)
    time_weight = gaussian(key_of[4], (3, C, 2 * C), (3 * C) ** -0.5, 0.1875)
    time_bias = gaussian(key_of[5], (2 * C,), 0.5, 3.0, (), jnp.float32)
    spatial_weight = gaussian(key_of[6], (3, 3, C, OUTC), (9 * C) ** -0.5, 0.109375)
    spatial_bias = gaussian(key_of[7], (OUTC,), 0.5, 3.0, (), jnp.float32)
    return dict(latents=latents, norm_gain=norm_gain, conv_weight=conv_weight, conv_bias=conv_bias, time_weight=time_weight, time_bias=time_bias, spatial_weight=spatial_weight, spatial_bias=spatial_bias)


def normalize_silu(values, gain):
    scale = lax.rsqrt(lax.optimization_barrier(jnp.mean(values * values, axis=-1, keepdims=True)) + 1e-06)
    return jax.nn.silu(values * scale * gain)

def reference(latents, norm_gain, conv_weight, conv_bias, time_weight, time_bias, spatial_weight, spatial_bias):
    widened = latents.astype(jnp.float32)
    activated = normalize_silu(widened, norm_gain).astype(jnp.bfloat16)
    padded = jnp.pad(activated.astype(jnp.float32), ((2, 0), (1, 1), (1, 1), (0, 0)))
    convolved = lax.conv_general_dilated(padded[None], conv_weight.astype(jnp.float32), (1, 1, 1), 'VALID', dimension_numbers=('NDHWC', 'DHWIO', 'NDHWC'), precision=lax.Precision.HIGHEST)[0]
    mixed = (convolved + conv_bias + widened).astype(jnp.bfloat16)
    mixed_pad = jnp.pad(mixed.astype(jnp.float32), ((2, 0), (0, 0), (0, 0), (0, 0)))
    frame_count = mixed.shape[0]
    running = time_bias
    for step_time in range(3):
        running = running + jnp.einsum('thwc,cd->thwd', mixed_pad[step_time:step_time + frame_count], time_weight[step_time].astype(jnp.float32), precision=lax.Precision.HIGHEST)
    doubled = running.astype(jnp.bfloat16)
    shape_in = doubled.shape
    halves = doubled.reshape(shape_in[0], shape_in[1], shape_in[2], 2, shape_in[3] // 2)
    frames_out = jnp.transpose(halves, (0, 3, 1, 2, 4)).reshape(2 * shape_in[0], shape_in[1], shape_in[2], shape_in[3] // 2)
    kernel = spatial_weight.astype(jnp.float32)

    def one_frame(single):
        enlarged = jnp.repeat(jnp.repeat(single, 2, axis=0), 2, axis=1).astype(jnp.float32)
        result = lax.conv_general_dilated(enlarged[None], kernel, (1, 1), ((1, 1), (1, 1)), dimension_numbers=('NHWC', 'HWIO', 'NHWC'), precision=lax.Precision.HIGHEST)[0]
        return (result + spatial_bias).astype(jnp.bfloat16)
    return lax.map(one_frame, frames_out)
```

```python
import jax
import jax.numpy as jnp
from jax import lax
from jax.experimental import pallas as pl
from jax.experimental.pallas import tpu as pltpu
from jax.sharding import PartitionSpec as P

F32 = jnp.float32
BF16 = jnp.bfloat16
HBM = pl.BlockSpec(memory_space=pltpu.HBM)
VMEM = pl.BlockSpec(memory_space=pltpu.VMEM)

C = 384
OUTC = 192
WIDE = 256
W = 32
OWN = 4
MROWS = 5
SIDE = 16
BLOCK = MROWS * W + SIDE
LIMIT = 24


def activate(values, gain):
    scale = lax.rsqrt(jnp.mean(values * values, axis=-1, keepdims=True) + 1e-06)
    half = values * scale * (0.5 * gain)
    return half + half * jnp.tanh(half)


def dot(left, right):
    return jnp.dot(left, right, preferred_element_type=F32)


def moved_columns(values, left, right):
    place = lax.broadcasted_iota(jnp.int32, values.shape, 0)
    before = jnp.where(place == 0, left, pltpu.roll(values, 1, 0))
    after = jnp.where(place == W - 1, right, pltpu.roll(values, W - 1, 0))
    return before.astype(BF16), values.astype(BF16), after.astype(BF16)


def slot_order(rows, core):
    place = lax.broadcasted_iota(jnp.int32, rows.shape, 0)
    upper = jnp.where(place == 0, 0.0, pltpu.roll(rows, 1, 0))
    lower = jnp.where(place >= 6, 0.0, pltpu.roll(rows, 6, 0))
    return jnp.where(core == 0, upper, lower)


def edge_kernel(own, other, edge, held):
    core = lax.axis_index("row")
    start = pl.multiple_of(core * 16, 16)
    for frame in range(4):
        for source, first in ((own, core * OWN), (other, OWN - core * OWN)):
            for row in range(OWN):
                values = source[frame, row, pl.ds(start, 16), :].astype(F32)
                values = jnp.where(core == 0, values, pltpu.roll(values, 2, 0))
                for col in range(2):
                    held[2 * frame + col, pl.ds(first + row, 1), :] = values[col : col + 1]
    for frame in range(4):
        for col in range(2):
            edge[frame, col] = held[2 * frame + col].astype(BF16)


def activate_kernel(own, other, gain, activated, edges):
    core = lax.axis_index("row")
    scale = gain[...].reshape(1, C)
    edges[...] = jnp.zeros(edges.shape, F32)

    def one(frame, carry):
        for slot in range(MROWS + 2):
            if slot == 0:
                values = other[frame, 2].astype(F32) * core.astype(F32)
            elif slot == 1:
                values = jnp.where(core == 0, own[frame, 0], other[frame, 3]).astype(F32)
            elif slot == 5:
                values = jnp.where(core == 0, other[frame, 0], own[frame, 3]).astype(F32)
            elif slot == 6:
                values = other[frame, 1].astype(F32) * (1 - core).astype(F32)
            else:
                values = own[frame, slot - 1 - core].astype(F32)
            values = activate(values, scale)
            edges[frame, 0, slot : slot + 1, :] = values[0:1]
            edges[frame, 1, slot : slot + 1, :] = values[W - 1 : W]
            activated[frame, slot] = values.astype(BF16)
        return carry

    lax.fori_loop(0, 4, one, 0)


def halo_columns(frame, mine, theirs, core):
    columns = []
    for col in range(4):
        first, second = (theirs, mine) if col < 2 else (mine, theirs)
        rows = jnp.where(core == 0, first[frame, col % 2], second[frame, col % 2]).astype(F32)
        columns.append(slot_order(rows, core))
    return columns


def fill_patches(frame, activated, edges, mine, theirs, gain, core, patches, line):
    columns = [activate(one, gain) for one in halo_columns(frame, mine, theirs, core)]
    line[frame, 0] = columns[1]
    line[frame, 1] = columns[2]
    at = frame * BLOCK
    for slot in range(MROWS + 2):
        moved = moved_columns(
            activated[frame, slot].astype(F32),
            line[frame, 0, slot : slot + 1, :],
            line[frame, 1, slot : slot + 1, :],
        )
        for tap_row in range(3):
            out_row = slot - tap_row
            if 0 <= out_row < MROWS:
                for tap_col in range(3):
                    tap = tap_row * 3 + tap_col
                    patches[at + out_row * W : at + (out_row + 1) * W, tap * C : (tap + 1) * C] = (
                        moved[tap_col]
                    )
    low = [columns[0], columns[1], edges[frame, 0]]
    high = [edges[frame, 1], columns[2], columns[3]]
    for tap_row in range(3):
        for tap_col in range(3):
            tap = tap_row * 3 + tap_col
            pair = [low[tap_col], high[tap_col]]
            if tap_row:
                pair = [pltpu.roll(one, 8 - tap_row, 0) for one in pair]
            patches[at + MROWS * W : at + BLOCK, tap * C : (tap + 1) * C] = jnp.concatenate(
                pair, axis=0
            ).astype(BF16)


def step_weight(weight, step):
    return weight[step].reshape(9 * C, C)


def send_kernel(
    activated, edges, mine, theirs, gain, weight, patches, onward, crossing, line
):
    core = lax.axis_index("row")
    scale = gain[...].reshape(1, C)
    for frame in (2, 3):
        fill_patches(frame, activated, edges, mine, theirs, scale, core, patches, line)
    both = jnp.concatenate([step_weight(weight, 0), step_weight(weight, 1)], axis=1)
    total = dot(patches[2 * BLOCK :], both)
    onward[0] = (total[:BLOCK, :C] + total[BLOCK:, C:]).astype(BF16)
    onward[1] = total[BLOCK:, :C].astype(BF16)
    crossing[...] = total[:BLOCK, C:]
    for frame in (0, 1):
        fill_patches(frame, activated, edges, mine, theirs, scale, core, patches, line)


def base_rows(frame, own, other, mine, theirs, bias, core):
    rows = []
    for out_row in range(MROWS):
        if out_row == 0:
            values = jnp.where(core == 0, own[frame, 0], other[frame, 3])
        elif out_row == OWN:
            values = jnp.where(core == 0, other[frame, 0], own[frame, 3])
        else:
            values = own[frame, out_row - core]
        rows.append(values.astype(F32) + bias)
    columns = halo_columns(frame, mine, theirs, core)
    rows.append(pltpu.roll(columns[1], 7, 0) + bias)
    rows.append(pltpu.roll(columns[2], 7, 0) + bias)
    return jnp.concatenate(rows, axis=0)


def own_kernel(
    patches, weight, crossing, own, other, mine, theirs, bias, mixed, early, late
):
    core = lax.axis_index("row")
    shift = bias[...].reshape(1, C)
    early[...] = dot(patches[: 2 * BLOCK], step_weight(weight, 0))
    late[...] = dot(patches[2 * BLOCK :], step_weight(weight, 2))
    middle = dot(patches[BLOCK : 2 * BLOCK], step_weight(weight, 1))
    third = base_rows(2, own, other, mine, theirs, shift, core)
    fourth = base_rows(3, own, other, mine, theirs, shift, core)
    mixed[0] = (third + early[:BLOCK] + late[:BLOCK] + middle).astype(BF16)
    mixed[1] = (fourth + early[BLOCK:] + late[BLOCK:] + crossing[...]).astype(BF16)


def upsampled(doubled, spatial, bias, last_col, framed, woven, out, target, frame0, sems):
    core = lax.axis_index("row")
    col = lax.axis_index("col")
    not_first = (col > 0).astype(F32)
    not_last = (col < last_col).astype(F32)
    for step in range(2):
        for half in range(2):
            lanes = slice(half * C, (half + 1) * C)
            for slot in range(MROWS + 1):
                row = jnp.clip(slot - 1 + core, 0, MROWS - 1)
                values = doubled[step, pl.ds(pl.multiple_of(row * W, W), W), lanes]
                left = doubled[step, pl.ds(MROWS * W + row, 1), lanes] * not_first
                right = doubled[step, pl.ds(MROWS * W + 8 + row, 1), lanes] * not_last
                if slot == 0 or slot == MROWS:
                    keep = core.astype(F32) if slot == 0 else (1 - core).astype(F32)
                    values, left, right = values * keep, left * keep, right * keep
                moved = moved_columns(values, left, right)
                for tap in range(3):
                    framed[2 * step + half, slot, :, tap * C : (tap + 1) * C] = moved[tap]
    shift = jnp.concatenate([bias[...].reshape(1, OUTC), jnp.zeros((1, WIDE - OUTC), F32)], axis=1)
    for parity_row in range(2):
        for parity_col in range(2):
            phase = parity_row * 2 + parity_col
            lanes = slice(parity_col * C, (parity_col + 2) * C)
            result = shift
            for near in range(2):
                rows = slice(parity_row + near, parity_row + near + OWN)
                result = result + lax.dot_general(
                    framed[:, rows, :, lanes].reshape(4 * OWN * W, 2 * C),
                    spatial[phase, near],
                    (((1,), (1,)), ((), ())),
                    preferred_element_type=F32,
                )
            for frame in range(4):
                for row in range(OWN):
                    start = (frame * OWN + row) * W
                    for lane in range(2):
                        woven[
                            lane, frame, 2 * row + parity_row, pl.ds(parity_col, W, stride=2), :
                        ] = result[start : start + W, lane * 128 : lane * 128 + 128]
    copies = []
    for frame in range(4):
        for row in range(2 * OWN):
            out[frame, row, :, :128] = woven[0, frame, row].astype(BF16)
            out[frame, row, :, 128:] = woven[1, frame, row][:, : OUTC - 128].astype(BF16)
        copies.append(
            pltpu.make_async_copy(out.at[frame], target.at[frame0 + frame], sems.at[frame])
        )
        copies[-1].start()
    for copy in copies:
        copy.wait()


def conv_time(frames, weight, bias, doubled):
    pair = [jnp.concatenate(frames[step : step + 3], axis=1) for step in range(2)]
    result = dot(
        jnp.concatenate(pair, axis=0), weight[...].reshape(3 * C, 2 * C)
    ) + bias[...].reshape(1, 2 * C)
    doubled[0] = result[:BLOCK]
    doubled[1] = result[BLOCK:]


def last_frames_kernel(
    last_col, patches, weight, own, other, mine, theirs, bias,
    onward, mixed, time, time_bias, spatial, spatial_bias,
    mixed_out, target,
    doubled, framed, woven, out, sems,
):
    core = lax.axis_index("row")
    shift = bias[...].reshape(1, C)
    late = dot(patches[: 2 * BLOCK], step_weight(weight, 2))
    middle = dot(patches[:BLOCK], step_weight(weight, 1))
    base = base_rows(0, own, other, mine, theirs, shift, core)
    first = (base + late[:BLOCK] + onward[0].astype(F32)).astype(BF16)
    base = base_rows(1, own, other, mine, theirs, shift, core)
    second = (base + late[BLOCK:] + middle + onward[1].astype(F32)).astype(BF16)
    mixed_out[0] = first
    mixed_out[1] = second
    conv_time([first, second, mixed[0], mixed[1]], time, time_bias, doubled)
    upsampled(doubled, spatial, spatial_bias, last_col, framed, woven, out, target, 4, sems)


def first_frames_kernel(
    last_col, previous, mixed, time, time_bias, spatial, spatial_bias, begun,
    target,
    doubled, framed, woven, out, sems,
):
    del begun
    conv_time([previous[0], previous[1], mixed[0], mixed[1]], time, time_bias, doubled)
    upsampled(doubled, spatial, spatial_bias, last_col, framed, woven, out, target, 0, sems)


def parity_kernel(weight, phases):
    for start in range(0, OUTC, 64):
        part = slice(start, start + 64)
        wide = [[weight[row, col, part, :].astype(F32) for col in range(3)] for row in range(3)]
        for parity_row in range(2):
            for near in range(2):
                first, last = ((0, 0), (1, 2)) if parity_row == 0 else ((0, 1), (2, 2))
                low, high = (first, last)[near]
                taps = wide[low]
                if high > low:
                    taps = [one + other for one, other in zip(wide[low], wide[high])]
                for parity_col in range(2):
                    phase = parity_row * 2 + parity_col
                    if parity_col == 0:
                        pair = [taps[0], taps[1] + taps[2]]
                    else:
                        pair = [taps[0] + taps[1], taps[2]]
                    for index in range(2):
                        phases[phase, near, part, index * C : (index + 1) * C] = pair[index].astype(
                            BF16
                        )
    for phase in range(4):
        for near in range(2):
            phases[phase, near, OUTC:, :] = jnp.zeros((WIDE - OUTC, 2 * C), BF16)


def cost(macs, bytes_accessed):
    return pl.CostEstimate(flops=2 * macs, bytes_accessed=bytes_accessed, transcendentals=0)


def call(kernel, name, estimate, limit=LIMIT, **rest):
    return pl.pallas_call(
        kernel,
        name=name,
        cost_estimate=estimate,
        compiler_params=pltpu.CompilerParams(vmem_limit_bytes=limit * 2**20),
        **rest,
    )


def swap_rows(block):
    return lax.ppermute(block, "row", [(0, 1), (1, 0)])


def to_later_frames(block):
    return lax.ppermute(block, "tm", [(i, i + 1) for i in range(lax.axis_size("tm") - 1)])


def across_columns(block):
    count = lax.axis_size("col")
    route = [(i, i - 1) for i in range(1, count)]
    route += [(count + i, count + i + 1) for i in range(count - 1)]
    return lax.ppermute(block, ("row", "col"), route)


def on_device(
    latents, norm_gain, conv_weight, conv_bias, time_weight, time_bias, spatial_weight, spatial_bias
):
    last_col = lax.axis_size("col") - 1
    other = swap_rows(latents)
    own = latents
    spatial_weight = jnp.swapaxes(spatial_weight, 2, 3)
    spatial = call(
        parity_kernel,
        "parity_weights",
        cost(2**30, 5 * 2**20),
        out_shape=jax.ShapeDtypeStruct((4, 2, WIDE, 2 * C), BF16),
        in_specs=[VMEM],
        out_specs=VMEM,
    )(spatial_weight)

    other, spatial = lax.optimization_barrier((other, spatial))
    edge = call(
        edge_kernel,
        "edge",
        cost(2**20, 2**20),
        out_shape=jax.ShapeDtypeStruct((4, 2, 8, C), BF16),
        in_specs=[VMEM] * 2,
        out_specs=VMEM,
        scratch_shapes=[pltpu.VMEM((8, 8, C), F32)],
    )(own, other)
    mine = across_columns(edge)

    activated, edges = call(
        activate_kernel,
        "activated",
        cost(2**32, 2**20),
        out_shape=(
            jax.ShapeDtypeStruct((4, MROWS + 2, W, C), BF16),
            jax.ShapeDtypeStruct((4, 2, 8, C), F32),
        ),
        in_specs=[VMEM] * 3,
        out_specs=(VMEM,) * 2,
    )(own, other, norm_gain)
    mine, activated = lax.optimization_barrier((mine, activated))
    theirs = swap_rows(mine)

    mixed_shape = jax.ShapeDtypeStruct((2, BLOCK, C), BF16)
    patches, onward, crossing = call(
        send_kernel,
        "partial_for_next",
        cost(4 * BLOCK * 9 * C * C, 10 * 2**20),
        out_shape=(
            jax.ShapeDtypeStruct((4 * BLOCK, 9 * C), BF16),
            mixed_shape,
            jax.ShapeDtypeStruct((BLOCK, C), F32),
        ),
        in_specs=[VMEM] * 6,
        out_specs=(VMEM,) * 3,
        scratch_shapes=[pltpu.VMEM((4, 2, 8, C), F32)],
    )(activated, edges, mine, theirs, norm_gain, conv_weight)
    onward = to_later_frames(onward)

    mixed = call(
        own_kernel,
        "mixed_last",
        cost(5 * BLOCK * 9 * C * C, 10 * 2**20),
        out_shape=mixed_shape,
        in_specs=[VMEM] * 8,
        out_specs=VMEM,
        scratch_shapes=[pltpu.VMEM((2 * BLOCK, C), F32), pltpu.VMEM((2 * BLOCK, C), F32)],
    )(patches, conv_weight, crossing, own, other, mine, theirs, conv_bias)
    previous = to_later_frames(mixed)

    out_shape = jax.ShapeDtypeStruct((8, 2 * OWN, 2 * W, OUTC), BF16)
    scratch = [
        pltpu.VMEM((2, BLOCK, 2 * C), F32),
        pltpu.VMEM((4, OWN + 2, W, 3 * C), BF16),
        pltpu.VMEM((2, 4, 2 * OWN, 2 * W, 128), F32),
        pltpu.VMEM((4, 2 * OWN, 2 * W, OUTC), BF16),
        pltpu.SemaphoreType.DMA((4,)),
    ]
    late_cost = cost(2 * BLOCK * 6 * C * C + 16 * 512 * C * WIDE, 6 * 2**20)

    def last_frames(*refs):
        last_frames_kernel(last_col, *refs)

    mixed_own, begun = call(
        last_frames,
        "upsample_last",
        late_cost,
        out_shape=(mixed_shape, out_shape),
        in_specs=[VMEM] * 13,
        out_specs=(VMEM, HBM),
        scratch_shapes=scratch,
    )(
        patches, conv_weight, own, other, mine, theirs, conv_bias,
        onward, mixed, time_weight, time_bias, spatial, spatial_bias,
    )

    def first_frames(*refs):
        first_frames_kernel(last_col, *refs)

    return call(
        first_frames,
        "upsample_first",
        late_cost,
        out_shape=out_shape,
        in_specs=[VMEM] * 6 + [HBM],
        out_specs=HBM,
        scratch_shapes=scratch,
        input_output_aliases={6: 0},
    )(previous, mixed_own, time_weight, time_bias, spatial, spatial_bias, begun)


def solution(mesh):
    placed = (P("tm", "row", "col", None), P(), P(), P(), P(), P(), P(), P())
    return jax.shard_map(
        on_device,
        mesh=mesh,
        in_specs=placed,
        out_specs=P("tm", "row", "col", None),
        check_vma=False,
    )
```

```python
import jax
import jax.numpy as jnp
from jax import lax
from jax.experimental import pallas as pl
from jax.experimental.pallas import tpu as pltpu
from jax.sharding import PartitionSpec as P

F32 = jnp.float32
BF16 = jnp.bfloat16
HBM = pl.BlockSpec(memory_space=pltpu.HBM)
VMEM = pl.BlockSpec(memory_space=pltpu.VMEM)

C = 384
OUTC = 192
WIDE = 256
W = 32
OWN = 4
MROWS = 5
SIDE = 16
BLOCK = MROWS * W + SIDE
LIMIT = 24


def activate(values, gain):
    scale = lax.rsqrt(jnp.mean(values * values, axis=-1, keepdims=True) + 1e-06)
    half = values * scale * (0.5 * gain)
    return half + half * jnp.tanh(half)


def dot(left, right):
    return jnp.dot(left, right, preferred_element_type=F32)


def moved_columns(values, left, right):
    place = lax.broadcasted_iota(jnp.int32, values.shape, 0)
    before = jnp.where(place == 0, left, pltpu.roll(values, 1, 0))
    after = jnp.where(place == W - 1, right, pltpu.roll(values, W - 1, 0))
    return before.astype(BF16), values.astype(BF16), after.astype(BF16)


def slot_order(rows, core):
    place = lax.broadcasted_iota(jnp.int32, rows.shape, 0)
    upper = jnp.where(place == 0, 0.0, pltpu.roll(rows, 1, 0))
    lower = jnp.where(place >= 6, 0.0, pltpu.roll(rows, 6, 0))
    return jnp.where(core == 0, upper, lower)


def cut_columns(source, first, core, held):
    start = pl.multiple_of(core * 16, 16)
    for frame in range(4):
        for row in range(OWN):
            values = source[frame, row, pl.ds(start, 16), :].astype(F32)
            values = jnp.where(core == 0, values, pltpu.roll(values, 2, 0))
            for col in range(2):
                held[2 * frame + col, pl.ds(first + row, 1), :] = values[col : col + 1]


def own_edge_kernel(own, held):
    core = lax.axis_index("row")
    cut_columns(own, core * OWN, core, held)


def edge_kernel(held, other, edge, rest):
    core = lax.axis_index("row")
    cut_columns(other, OWN - core * OWN, core, rest)
    place = lax.broadcasted_iota(jnp.int32, (8, C), 0)
    mine = (place < OWN) == (core == 0)
    for frame in range(4):
        for col in range(2):
            index = 2 * frame + col
            edge[frame, col] = jnp.where(mine, held[index], rest[index]).astype(BF16)


def activate_kernel(
    own, other, gain, weight, activated, edges, third, first, third_patches, first_patches
):
    core = lax.axis_index("row")
    scale = gain[...].reshape(1, C)
    edges[...] = jnp.zeros(edges.shape, F32)

    def one(frame, carry):
        for slot in range(MROWS + 2):
            if slot == 0:
                values = other[frame, 2].astype(F32) * core.astype(F32)
            elif slot == 1:
                values = jnp.where(core == 0, own[frame, 0], other[frame, 3]).astype(F32)
            elif slot == 5:
                values = jnp.where(core == 0, other[frame, 0], own[frame, 3]).astype(F32)
            elif slot == 6:
                values = other[frame, 1].astype(F32) * (1 - core).astype(F32)
            else:
                values = own[frame, slot - 1 - core].astype(F32)
            values = activate(values, scale)
            edges[frame, 0, slot : slot + 1, :] = values[0:1]
            edges[frame, 1, slot : slot + 1, :] = values[W - 1 : W]
            activated[frame, slot] = values.astype(BF16)
        return carry

    lax.fori_loop(0, 4, one, 0)
    inner_products(3, activated, weight, third_patches, third)
    inner_products(1, activated, weight, first_patches, first)


def inner_kernel(activated, weight, total, patches):
    inner_products(2, activated, weight, patches, total)


def halo_columns(frame, mine, theirs, core):
    columns = []
    for col in range(4):
        first, second = (theirs, mine) if col < 2 else (mine, theirs)
        rows = jnp.where(core == 0, first[frame, col % 2], second[frame, col % 2]).astype(F32)
        columns.append(slot_order(rows, core))
    return columns


def fill_rows(at, slot, values, left, right, patches):
    moved = moved_columns(values, left, right)
    for tap_row in range(3):
        out_row = slot - tap_row
        if 0 <= out_row < MROWS:
            for tap_col in range(3):
                tap = tap_row * 3 + tap_col
                patches[at + out_row * W : at + (out_row + 1) * W, tap * C : (tap + 1) * C] = moved[
                    tap_col
                ]


def fill_patches(frame, at, activated, edges, columns, patches, line):
    line[frame, 0] = columns[1]
    line[frame, 1] = columns[2]
    for slot in range(MROWS + 2):
        left = line[frame, 0, slot : slot + 1, :]
        right = line[frame, 1, slot : slot + 1, :]
        fill_rows(at, slot, activated[frame, slot].astype(F32), left, right, patches)
    fill_sides(at + MROWS * W, frame, edges, columns, patches, False)


def fill_sides(at, frame, edges, columns, patches, inner):
    low = [columns[0], columns[1], edges[frame, 0]]
    high = [edges[frame, 1], columns[2], columns[3]]
    none = jnp.zeros((8, C), F32)
    for tap_row in range(3):
        for tap_col in range(3):
            tap = tap_row * 3 + tap_col
            parts = [low[tap_col], high[tap_col]]
            if inner:
                parts.append(columns[1] if tap_col == 0 else none)
                parts.append(columns[2] if tap_col == 2 else none)
            if tap_row:
                parts = [pltpu.roll(one, 8 - tap_row, 0) for one in parts]
            rows = slice(at, at + 8 * len(parts))
            patches[rows, tap * C : (tap + 1) * C] = jnp.concatenate(parts, axis=0).astype(BF16)


def early_weight(weight):
    return jnp.concatenate([step_weight(weight, 0), step_weight(weight, 1)], axis=1)


def inner_products(frame, activated, weight, patches, total):
    for slot in range(MROWS + 2):
        fill_rows(0, slot, activated[frame, slot].astype(F32), 0.0, 0.0, patches)
    total[...] = dot(patches[...], early_weight(weight))


def step_weight(weight, step):
    return weight[step].reshape(9 * C, C)


def outer_columns(frame, mine, theirs, gain, core):
    return [activate(one, gain) for one in halo_columns(frame, mine, theirs, core)]


def send_kernel(
    edges, mine, theirs, gain, weight, inner1, inner2, inner3, onward, crossing, sides, total
):
    core = lax.axis_index("row")
    scale = gain[...].reshape(1, C)
    for index in range(3):
        columns = outer_columns(1 + index, mine, theirs, scale, core)
        fill_sides(index * 32, 1 + index, edges, columns, sides, True)
    extra = dot(sides[...], early_weight(weight))
    for index, inner in enumerate((inner1, inner2, inner3)):
        base = index * 32
        total[index, : MROWS * W] = inner[...]
        total[index, MROWS * W :] = extra[base : base + SIDE]
        for row in range(MROWS):
            for at, side in ((row * W, 16), (row * W + W - 1, 24)):
                line = slice(at, at + 1)
                add = slice(base + side + row, base + side + row + 1)
                total[index, line] = inner[line] + extra[add]
    onward[0] = (total[1, :, :C] + total[2, :, C:]).astype(BF16)
    onward[1] = total[2, :, :C].astype(BF16)
    crossing[0] = total[0, :, C:]
    crossing[1] = total[0, :, :C] + total[1, :, C:]


def base_rows(frame, own, other, mine, theirs, bias, core):
    rows = []
    for out_row in range(MROWS):
        if out_row == 0:
            values = jnp.where(core == 0, own[frame, 0], other[frame, 3])
        elif out_row == OWN:
            values = jnp.where(core == 0, other[frame, 0], own[frame, 3])
        else:
            values = own[frame, out_row - core]
        rows.append(values.astype(F32) + bias)
    columns = halo_columns(frame, mine, theirs, core)
    rows.append(pltpu.roll(columns[1], 7, 0) + bias)
    rows.append(pltpu.roll(columns[2], 7, 0) + bias)
    return jnp.concatenate(rows, axis=0)


def own_kernel(
    activated, edges, gain, weight, crossing, own, other, mine, theirs, bias, mixed, patches,
    last_patches, line,
):
    core = lax.axis_index("row")
    shift = bias[...].reshape(1, C)
    scale = gain[...].reshape(1, C)

    def fill(frame, target, at):
        columns = outer_columns(frame, mine, theirs, scale, core)
        fill_patches(frame, at, activated, edges, columns, target, line)

    fill(2, last_patches, 0)
    fill(3, last_patches, BLOCK)
    late = dot(last_patches[...], step_weight(weight, 2))
    fill(0, patches, 0)
    early = dot(patches[...], step_weight(weight, 0))
    fourth = base_rows(3, own, other, mine, theirs, shift, core)
    mixed[1] = (fourth + late[BLOCK:] + crossing[1]).astype(BF16)
    third = base_rows(2, own, other, mine, theirs, shift, core)
    mixed[0] = (third + late[:BLOCK] + crossing[0] + early).astype(BF16)


def first_part_kernel(
    patches, activated, edges, gain, weight, own, other, mine, theirs, bias, spatial_weight,
    part, spatial,
    second_patches, line,
):
    core = lax.axis_index("row")
    shift = bias[...].reshape(1, C)
    scale = gain[...].reshape(1, C)
    both = jnp.concatenate([step_weight(weight, 1), step_weight(weight, 2)], axis=1)
    early = dot(patches[...], both)
    parity_weights(spatial_weight, spatial)
    columns = outer_columns(1, mine, theirs, scale, core)
    fill_patches(1, 0, activated, edges, columns, second_patches, line)
    part[0] = base_rows(0, own, other, mine, theirs, shift, core) + early[:, C:]
    late = dot(second_patches[...], step_weight(weight, 2))
    part[1] = base_rows(1, own, other, mine, theirs, shift, core) + early[:, :C] + late


def frame_step(doubled, last_col, framed):
    core = lax.axis_index("row")
    col = lax.axis_index("col")
    not_first = (col > 0).astype(F32)
    not_last = (col < last_col).astype(F32)
    for half in range(2):
        lanes = slice(half * C, (half + 1) * C)

        def row_of(row):
            return (
                doubled[row * W : (row + 1) * W, lanes],
                doubled[MROWS * W + row : MROWS * W + row + 1, lanes] * not_first,
                doubled[MROWS * W + 8 + row : MROWS * W + 9 + row, lanes] * not_last,
            )

        for slot in range(MROWS + 1):
            if slot == 0:
                parts = [jnp.where(core == 0, 0.0, one) for one in row_of(0)]
            elif slot == MROWS:
                parts = [jnp.where(core == 0, one, 0.0) for one in row_of(MROWS - 1)]
            else:
                pairs = zip(row_of(slot - 1), row_of(slot))
                parts = [jnp.where(core == 0, upper, lower) for upper, lower in pairs]
            moved = moved_columns(*parts)
            for tap in range(3):
                framed[half, slot, :, tap * C : (tap + 1) * C] = moved[tap]


def spatial_step(framed, spatial, bias, woven):
    shift = jnp.concatenate([bias[...].reshape(1, OUTC), jnp.zeros((1, WIDE - OUTC), F32)], axis=1)
    for parity_row in range(2):
        for parity_col in range(2):
            phase = parity_row * 2 + parity_col
            lanes = slice(parity_col * C, (parity_col + 2) * C)
            result = shift
            for near in range(2):
                rows = slice(parity_row + near, parity_row + near + OWN)
                result = result + lax.dot_general(
                    framed[:, rows, :, lanes].reshape(2 * OWN * W, 2 * C),
                    spatial[phase, near],
                    (((1,), (1,)), ((), ())),
                    preferred_element_type=F32,
                )
            for frame in range(2):
                for row in range(OWN):
                    start = (frame * OWN + row) * W
                    for lane in range(2):
                        woven[
                            lane, frame, 2 * row + parity_row, pl.ds(parity_col, W, stride=2), :
                        ] = result[start : start + W, lane * 128 : lane * 128 + 128]


def weave_step(woven, out, target, frame0, sems):
    copies = []
    for frame in range(2):
        for row in range(2 * OWN):
            out[frame, row, :, :128] = woven[0, frame, row].astype(BF16)
            out[frame, row, :, 128:] = woven[1, frame, row][:, : OUTC - 128].astype(BF16)
        copies.append(
            pltpu.make_async_copy(out.at[frame], target.at[frame0 + frame], sems.at[frame])
        )
        copies[-1].start()
    return copies


def upsampled(last_col, spatial, bias, target, frame0, first, second):
    frame_step(first[0], last_col, first[1])
    spatial_step(first[1], spatial, bias, first[2])
    frame_step(second[0], last_col, second[1])
    spatial_step(second[1], spatial, bias, second[2])
    copies = weave_step(first[2], first[3], target, frame0, first[4])
    copies += weave_step(second[2], second[3], target, frame0 + 2, second[4])
    for copy in copies:
        copy.wait()


def last_frames_kernel(
    last_col, part, onward, mixed, time, time_bias, spatial, spatial_bias, begun, target, *scratch
):
    first_half, second_half = scratch[:5], scratch[5:]
    first = (part[0] + onward[0].astype(F32)).astype(BF16)
    second = (part[1] + onward[1].astype(F32)).astype(BF16)
    whole = time[...].reshape(3 * C, 2 * C)
    shift = time_bias[...].reshape(1, 2 * C)
    first_half[0][...] = (
        dot(jnp.concatenate([first, second, mixed[0]], axis=1), whole) + shift
    )
    second_half[0][...] = (
        dot(jnp.concatenate([second, mixed[0], mixed[1]], axis=1), whole) + shift
    )
    begun[0] = dot(first, whole[2 * C :]) + shift
    begun[1] = dot(jnp.concatenate([first, second], axis=1), whole[C:]) + shift
    upsampled(last_col, spatial, spatial_bias, target, 4, first_half, second_half)


def first_frames_kernel(
    last_col, previous, begun, time, spatial, spatial_bias, half_done, target, *scratch
):
    del half_done
    first_half, second_half = scratch[:5], scratch[5:]
    whole = time[...].reshape(3 * C, 2 * C)
    first_half[0][...] = begun[0] + dot(
        jnp.concatenate([previous[0], previous[1]], axis=1), whole[: 2 * C]
    )
    second_half[0][...] = begun[1] + dot(previous[1], whole[:C])
    upsampled(last_col, spatial, spatial_bias, target, 0, first_half, second_half)


def parity_weights(weight, phases):
    for start in range(0, OUTC, 64):
        part = slice(start, start + 64)
        wide = [[weight[row, col, part, :].astype(F32) for col in range(3)] for row in range(3)]
        for parity_row in range(2):
            for near in range(2):
                first, last = ((0, 0), (1, 2)) if parity_row == 0 else ((0, 1), (2, 2))
                low, high = (first, last)[near]
                taps = wide[low]
                if high > low:
                    taps = [one + other for one, other in zip(wide[low], wide[high])]
                for parity_col in range(2):
                    phase = parity_row * 2 + parity_col
                    if parity_col == 0:
                        pair = [taps[0], taps[1] + taps[2]]
                    else:
                        pair = [taps[0] + taps[1], taps[2]]
                    for index in range(2):
                        phases[phase, near, part, index * C : (index + 1) * C] = pair[index].astype(
                            BF16
                        )
    for phase in range(4):
        for near in range(2):
            phases[phase, near, OUTC:, :] = jnp.zeros((WIDE - OUTC, 2 * C), BF16)


def cost(macs, bytes_accessed):
    return pl.CostEstimate(flops=2 * macs, bytes_accessed=bytes_accessed, transcendentals=0)


def call(kernel, name, estimate, limit=LIMIT, **rest):
    return pl.pallas_call(
        kernel,
        name=name,
        cost_estimate=estimate,
        compiler_params=pltpu.CompilerParams(vmem_limit_bytes=limit * 2**20),
        **rest,
    )


def swap_rows(block):
    return lax.ppermute(block, "row", [(0, 1), (1, 0)])


def to_later_frames(block):
    return lax.ppermute(block, "tm", [(i, i + 1) for i in range(lax.axis_size("tm") - 1)])


def across_columns(block):
    count = lax.axis_size("col")
    route = [(i, i - 1) for i in range(1, count)]
    route += [(count + i, count + i + 1) for i in range(count - 1)]
    return lax.ppermute(block, ("row", "col"), route)


def on_device(
    latents, norm_gain, conv_weight, conv_bias, time_weight, time_bias, spatial_weight, spatial_bias
):
    last_col = lax.axis_size("col") - 1
    other = swap_rows(latents)
    own = latents
    spatial_weight = jnp.swapaxes(spatial_weight, 2, 3)
    held = call(
        own_edge_kernel,
        "own_edge",
        cost(2**33, 2**20),
        out_shape=jax.ShapeDtypeStruct((8, 8, C), F32),
        in_specs=[VMEM],
        out_specs=VMEM,
    )(own)
    edge = call(
        edge_kernel,
        "edge",
        cost(2**33, 2**20),
        out_shape=jax.ShapeDtypeStruct((4, 2, 8, C), BF16),
        in_specs=[VMEM] * 2,
        out_specs=VMEM,
        scratch_shapes=[pltpu.VMEM((8, 8, C), F32)],
    )(held, other)
    mine = across_columns(edge)

    inner_shape = jax.ShapeDtypeStruct((MROWS * W, 2 * C), F32)
    inner_patches = pltpu.VMEM((MROWS * W, 9 * C), BF16)
    inner_cost = cost(2 * MROWS * W * 9 * C * C, 7 * 2**20)
    activated, edges, inner3, inner1 = call(
        activate_kernel,
        "activated",
        cost(4 * MROWS * W * 9 * C * C, 7 * 2**20),
        out_shape=(
            jax.ShapeDtypeStruct((4, MROWS + 2, W, C), BF16),
            jax.ShapeDtypeStruct((4, 2, 8, C), F32),
            inner_shape,
            inner_shape,
        ),
        in_specs=[VMEM] * 4,
        out_specs=(VMEM,) * 4,
        scratch_shapes=[inner_patches, inner_patches],
    )(own, other, norm_gain, conv_weight)
    mine, activated = lax.optimization_barrier((mine, activated))
    theirs = swap_rows(mine)
    inner2 = call(
        inner_kernel,
        "inner",
        inner_cost,
        out_shape=inner_shape,
        in_specs=[VMEM] * 2,
        out_specs=VMEM,
        scratch_shapes=[inner_patches],
    )(activated, conv_weight)

    mixed_shape = jax.ShapeDtypeStruct((2, BLOCK, C), BF16)
    onward, crossing = call(
        send_kernel,
        "partial_for_next",
        cost(2 * 96 * 9 * C * C, 10 * 2**20),
        out_shape=(mixed_shape, jax.ShapeDtypeStruct((2, BLOCK, C), F32)),
        in_specs=[VMEM] * 8,
        out_specs=(VMEM,) * 2,
        scratch_shapes=[pltpu.VMEM((96, 9 * C), BF16), pltpu.VMEM((3, BLOCK, 2 * C), F32)],
    )(edges, mine, theirs, norm_gain, conv_weight, inner1, inner2, inner3)
    onward = to_later_frames(onward)

    line = pltpu.VMEM((4, 2, 8, C), F32)
    mixed, patches = call(
        own_kernel,
        "mixed_last",
        cost(3 * BLOCK * 9 * C * C, 10 * 2**20),
        out_shape=(mixed_shape, jax.ShapeDtypeStruct((BLOCK, 9 * C), BF16)),
        in_specs=[VMEM] * 10,
        out_specs=(VMEM,) * 2,
        scratch_shapes=[pltpu.VMEM((2 * BLOCK, 9 * C), BF16), line],
    )(activated, edges, norm_gain, conv_weight, crossing, own, other, mine, theirs, conv_bias)
    previous = to_later_frames(mixed)

    out_shape = jax.ShapeDtypeStruct((8, 2 * OWN, 2 * W, OUTC), BF16)
    scratch = 2 * [
        pltpu.VMEM((BLOCK, 2 * C), F32),
        pltpu.VMEM((2, OWN + 2, W, 3 * C), BF16),
        pltpu.VMEM((2, 2, 2 * OWN, 2 * W, 128), F32),
        pltpu.VMEM((2, 2 * OWN, 2 * W, OUTC), BF16),
        pltpu.SemaphoreType.DMA((2,)),
    ]
    late_cost = cost(2 * BLOCK * 6 * C * C + 16 * 512 * C * WIDE, 6 * 2**20)

    part, spatial = call(
        first_part_kernel,
        "mixed_first",
        cost(3 * BLOCK * 9 * C * C, 10 * 2**20),
        out_shape=(
            jax.ShapeDtypeStruct((2, BLOCK, C), F32),
            jax.ShapeDtypeStruct((4, 2, WIDE, 2 * C), BF16),
        ),
        in_specs=[VMEM] * 11,
        out_specs=(VMEM,) * 2,
        scratch_shapes=[pltpu.VMEM((BLOCK, 9 * C), BF16), line],
    )(
        patches, activated, edges, norm_gain, conv_weight, own, other, mine, theirs, conv_bias,
        spatial_weight,
    )

    def last_frames(*refs):
        last_frames_kernel(last_col, *refs)

    begun, half_done = call(
        last_frames,
        "upsample_last",
        late_cost,
        out_shape=(jax.ShapeDtypeStruct((2, BLOCK, 2 * C), F32), out_shape),
        in_specs=[VMEM] * 7,
        out_specs=(VMEM, HBM),
        scratch_shapes=scratch,
    )(part, onward, mixed, time_weight, time_bias, spatial, spatial_bias)

    def first_frames(*refs):
        first_frames_kernel(last_col, *refs)

    return call(
        first_frames,
        "upsample_first",
        late_cost,
        out_shape=out_shape,
        in_specs=[VMEM] * 5 + [HBM],
        out_specs=HBM,
        scratch_shapes=scratch,
        input_output_aliases={5: 0},
    )(previous, begun, time_weight, spatial, spatial_bias, half_done)


def solution(mesh):
    placed = (P("tm", "row", "col", None), P(), P(), P(), P(), P(), P(), P())
    return jax.shard_map(
        on_device,
        mesh=mesh,
        in_specs=placed,
        out_specs=P("tm", "row", "col", None),
        check_vma=False,
    )
```

```python
import jax
import jax.numpy as jnp
from jax import lax
from jax.experimental import pallas as pl
from jax.experimental.pallas import tpu as pltpu
from jax.sharding import PartitionSpec as P

F32 = jnp.float32
BF16 = jnp.bfloat16
HBM = pl.BlockSpec(memory_space=pltpu.HBM)
VMEM = pl.BlockSpec(memory_space=pltpu.VMEM)

C = 384
OUTC = 192
WIDE = 256
W = 32
OWN = 4
MROWS = 5
SIDE = 16
BLOCK = MROWS * W + SIDE
LIMIT = 24


def activate(values, gain):
    scale = lax.rsqrt(jnp.mean(values * values, axis=-1, keepdims=True) + 1e-06)
    half = values * scale * (0.5 * gain)
    return half + half * jnp.tanh(half)


def dot(left, right):
    return jnp.dot(left, right, preferred_element_type=F32)


def moved_columns(values, left, right):
    place = lax.broadcasted_iota(jnp.int32, values.shape, 0)
    before = jnp.where(place == 0, left, pltpu.roll(values, 1, 0))
    after = jnp.where(place == W - 1, right, pltpu.roll(values, W - 1, 0))
    return before.astype(BF16), values.astype(BF16), after.astype(BF16)


def slot_order(rows, core):
    place = lax.broadcasted_iota(jnp.int32, rows.shape, 0)
    upper = jnp.where(place == 0, 0.0, pltpu.roll(rows, 1, 0))
    lower = jnp.where(place >= 6, 0.0, pltpu.roll(rows, 6, 0))
    return jnp.where(core == 0, upper, lower)


def cut_columns(source, first, core, held):
    start = pl.multiple_of(core * 16, 16)
    for frame in range(4):
        for row in range(OWN):
            values = source[frame, row, pl.ds(start, 16), :].astype(F32)
            values = jnp.where(core == 0, values, pltpu.roll(values, 2, 0))
            for col in range(2):
                held[2 * frame + col, pl.ds(first + row, 1), :] = values[col : col + 1]


def own_edge_kernel(own, held):
    core = lax.axis_index("row")
    cut_columns(own, core * OWN, core, held)


def edge_kernel(held, other, edge, rest):
    core = lax.axis_index("row")
    cut_columns(other, OWN - core * OWN, core, rest)
    place = lax.broadcasted_iota(jnp.int32, (8, C), 0)
    mine = (place < OWN) == (core == 0)
    for frame in range(4):
        for col in range(2):
            index = 2 * frame + col
            edge[frame, col] = jnp.where(mine, held[index], rest[index]).astype(BF16)


def activate_kernel(
    own, other, gain, weight, activated, edges, third, first, third_patches, first_patches
):
    core = lax.axis_index("row")
    scale = gain[...].reshape(1, C)
    edges[...] = jnp.zeros(edges.shape, F32)

    def one(frame):
        for slot in range(MROWS + 2):
            if slot == 0:
                values = other[frame, 2].astype(F32) * core.astype(F32)
            elif slot == 1:
                values = jnp.where(core == 0, own[frame, 0], other[frame, 3]).astype(F32)
            elif slot == 5:
                values = jnp.where(core == 0, other[frame, 0], own[frame, 3]).astype(F32)
            elif slot == 6:
                values = other[frame, 1].astype(F32) * (1 - core).astype(F32)
            else:
                values = own[frame, slot - 1 - core].astype(F32)
            values = activate(values, scale)
            edges[frame, 0, slot : slot + 1, :] = values[0:1]
            edges[frame, 1, slot : slot + 1, :] = values[W - 1 : W]
            activated[frame, slot] = values.astype(BF16)

    one(3)
    inner_products(3, activated, weight, third_patches, third)
    one(1)
    inner_products(1, activated, weight, first_patches, first)
    one(0)
    one(2)


def inner_kernel(activated, weight, total, patches):
    inner_products(2, activated, weight, patches, total)


def halo_columns(frame, mine, theirs, core):
    columns = []
    for col in range(4):
        first, second = (theirs, mine) if col < 2 else (mine, theirs)
        rows = jnp.where(core == 0, first[frame, col % 2], second[frame, col % 2]).astype(F32)
        columns.append(slot_order(rows, core))
    return columns


def fill_rows(at, slot, values, left, right, patches):
    moved = moved_columns(values, left, right)
    for tap_row in range(3):
        out_row = slot - tap_row
        if 0 <= out_row < MROWS:
            for tap_col in range(3):
                tap = tap_row * 3 + tap_col
                patches[at + out_row * W : at + (out_row + 1) * W, tap * C : (tap + 1) * C] = moved[
                    tap_col
                ]


def fill_patches(frame, at, activated, edges, outer, patches):
    columns = [outer[frame, index] for index in range(4)]
    for slot in range(MROWS + 2):
        left = outer[frame, 1, slot : slot + 1, :]
        right = outer[frame, 2, slot : slot + 1, :]
        fill_rows(at, slot, activated[frame, slot].astype(F32), left, right, patches)
    fill_sides(at + MROWS * W, frame, edges, columns, patches, False)


def fill_sides(at, frame, edges, columns, patches, inner):
    low = [columns[0], columns[1], edges[frame, 0]]
    high = [edges[frame, 1], columns[2], columns[3]]
    none = jnp.zeros((8, C), F32)
    for tap_row in range(3):
        for tap_col in range(3):
            tap = tap_row * 3 + tap_col
            parts = [low[tap_col], high[tap_col]]
            if inner:
                parts.append(columns[1] if tap_col == 0 else none)
                parts.append(columns[2] if tap_col == 2 else none)
            if tap_row:
                parts = [pltpu.roll(one, 8 - tap_row, 0) for one in parts]
            rows = slice(at, at + 8 * len(parts))
            patches[rows, tap * C : (tap + 1) * C] = jnp.concatenate(parts, axis=0).astype(BF16)


def early_weight(weight):
    return jnp.concatenate([step_weight(weight, 0), step_weight(weight, 1)], axis=1)


def inner_products(frame, activated, weight, patches, total):
    for slot in range(MROWS + 2):
        fill_rows(0, slot, activated[frame, slot].astype(F32), 0.0, 0.0, patches)
    total[...] = dot(patches[...], early_weight(weight))


def step_weight(weight, step):
    return weight[step].reshape(9 * C, C)


def outer_columns(frame, mine, theirs, gain, core):
    return [activate(one, gain) for one in halo_columns(frame, mine, theirs, core)]


def send_kernel(
    edges, mine, theirs, gain, weight, inner1, inner2, inner3, onward, crossing, outer, sides, total
):
    core = lax.axis_index("row")
    scale = gain[...].reshape(1, C)
    for frame in (1, 2, 3):
        columns = outer_columns(frame, mine, theirs, scale, core)
        for index in range(4):
            outer[frame, index] = columns[index]
        fill_sides((frame - 1) * 32, frame, edges, columns, sides, True)
    extra = dot(sides[...], early_weight(weight))
    columns = outer_columns(0, mine, theirs, scale, core)
    for index in range(4):
        outer[0, index] = columns[index]
    for index, inner in enumerate((inner1, inner2, inner3)):
        base = index * 32
        total[index, : MROWS * W] = inner[...]
        total[index, MROWS * W :] = extra[base : base + SIDE]
        for row in range(MROWS):
            for at, side in ((row * W, 16), (row * W + W - 1, 24)):
                line = slice(at, at + 1)
                add = slice(base + side + row, base + side + row + 1)
                total[index, line] = inner[line] + extra[add]
    onward[0] = (total[1, :, :C] + total[2, :, C:]).astype(BF16)
    onward[1] = total[2, :, :C].astype(BF16)
    crossing[0] = total[0, :, C:]
    crossing[1] = total[0, :, :C] + total[1, :, C:]


def base_rows(frame, own, other, mine, theirs, bias, core):
    rows = []
    for out_row in range(MROWS):
        if out_row == 0:
            values = jnp.where(core == 0, own[frame, 0], other[frame, 3])
        elif out_row == OWN:
            values = jnp.where(core == 0, other[frame, 0], own[frame, 3])
        else:
            values = own[frame, out_row - core]
        rows.append(values.astype(F32) + bias)
    columns = halo_columns(frame, mine, theirs, core)
    rows.append(pltpu.roll(columns[1], 7, 0) + bias)
    rows.append(pltpu.roll(columns[2], 7, 0) + bias)
    return jnp.concatenate(rows, axis=0)


def own_kernel(
    activated, edges, outer, weight, crossing, own, other, mine, theirs, bias, mixed, patches,
    third_patches, fourth_patches,
):
    core = lax.axis_index("row")
    shift = bias[...].reshape(1, C)
    fill_patches(3, 0, activated, edges, outer, fourth_patches)
    late = dot(fourth_patches[...], step_weight(weight, 2))
    fill_patches(2, 0, activated, edges, outer, third_patches)
    fourth = base_rows(3, own, other, mine, theirs, shift, core)
    mixed[1] = (fourth + late + crossing[1]).astype(BF16)
    late = dot(third_patches[...], step_weight(weight, 2))
    fill_patches(0, 0, activated, edges, outer, patches)
    third = base_rows(2, own, other, mine, theirs, shift, core)
    early = dot(patches[...], step_weight(weight, 0))
    mixed[0] = (third + late + crossing[0] + early).astype(BF16)


def first_part_kernel(
    patches, activated, edges, outer, weight, own, other, mine, theirs, bias, spatial_weight,
    part, spatial,
    second_patches,
):
    core = lax.axis_index("row")
    shift = bias[...].reshape(1, C)
    both = jnp.concatenate([step_weight(weight, 1), step_weight(weight, 2)], axis=1)
    early = dot(patches[...], both)
    parity_weights(spatial_weight, spatial)
    fill_patches(1, 0, activated, edges, outer, second_patches)
    part[0] = base_rows(0, own, other, mine, theirs, shift, core) + early[:, C:]
    late = dot(second_patches[...], step_weight(weight, 2))
    part[1] = base_rows(1, own, other, mine, theirs, shift, core) + early[:, :C] + late


def frame_step(doubled, last_col, framed):
    core = lax.axis_index("row")
    col = lax.axis_index("col")
    not_first = (col > 0).astype(F32)
    not_last = (col < last_col).astype(F32)
    for half in range(2):
        lanes = slice(half * C, (half + 1) * C)

        def row_of(row):
            return (
                doubled[row * W : (row + 1) * W, lanes],
                doubled[MROWS * W + row : MROWS * W + row + 1, lanes] * not_first,
                doubled[MROWS * W + 8 + row : MROWS * W + 9 + row, lanes] * not_last,
            )

        for slot in range(MROWS + 1):
            if slot == 0:
                parts = [jnp.where(core == 0, 0.0, one) for one in row_of(0)]
            elif slot == MROWS:
                parts = [jnp.where(core == 0, one, 0.0) for one in row_of(MROWS - 1)]
            else:
                pairs = zip(row_of(slot - 1), row_of(slot))
                parts = [jnp.where(core == 0, upper, lower) for upper, lower in pairs]
            moved = moved_columns(*parts)
            for tap in range(3):
                framed[half, slot, :, tap * C : (tap + 1) * C] = moved[tap]


def spatial_step(framed, spatial, bias, woven):
    shift = jnp.concatenate([bias[...].reshape(1, OUTC), jnp.zeros((1, WIDE - OUTC), F32)], axis=1)
    for parity_row in range(2):
        for parity_col in range(2):
            phase = parity_row * 2 + parity_col
            lanes = slice(parity_col * C, (parity_col + 2) * C)
            result = shift
            for near in range(2):
                rows = slice(parity_row + near, parity_row + near + OWN)
                result = result + dot(
                    framed[:, rows, :, lanes].reshape(2 * OWN * W, 2 * C),
                    spatial[phase, near],
                )
            for frame in range(2):
                for row in range(OWN):
                    start = (frame * OWN + row) * W
                    for lane in range(2):
                        woven[
                            lane, frame, 2 * row + parity_row, pl.ds(parity_col, W, stride=2), :
                        ] = result[start : start + W, lane * 128 : lane * 128 + 128]


def weave_step(woven, out, target, frame0, sems):
    copies = []
    for frame in range(2):
        for row in range(2 * OWN):
            out[frame, row, :, :128] = woven[0, frame, row].astype(BF16)
            out[frame, row, :, 128:] = woven[1, frame, row][:, : OUTC - 128].astype(BF16)
        copies.append(
            pltpu.make_async_copy(out.at[frame], target.at[frame0 + frame], sems.at[frame])
        )
        copies[-1].start()
    return copies


def upsampled(last_col, spatial, bias, target, frame0, first, second):
    frame_step(first[0], last_col, first[1])
    spatial_step(first[1], spatial, bias, first[2])
    frame_step(second[0], last_col, second[1])
    spatial_step(second[1], spatial, bias, second[2])
    copies = weave_step(first[2], first[3], target, frame0, first[4])
    copies += weave_step(second[2], second[3], target, frame0 + 2, second[4])
    for copy in copies:
        copy.wait()


def last_frames_kernel(
    last_col, part, onward, mixed, time, time_bias, spatial, spatial_bias, begun, target, *scratch
):
    first_half, second_half = scratch[:5], scratch[5:]
    first = (part[0] + onward[0].astype(F32)).astype(BF16)
    second = (part[1] + onward[1].astype(F32)).astype(BF16)
    whole = time[...].reshape(3 * C, 2 * C)
    shift = time_bias[...].reshape(1, 2 * C)
    first_half[0][...] = (
        dot(jnp.concatenate([first, second, mixed[0]], axis=1), whole) + shift
    )
    second_half[0][...] = (
        dot(jnp.concatenate([second, mixed[0], mixed[1]], axis=1), whole) + shift
    )
    begun[0] = dot(first, whole[2 * C :]) + shift
    begun[1] = dot(jnp.concatenate([first, second], axis=1), whole[C:]) + shift
    upsampled(last_col, spatial, spatial_bias, target, 4, first_half, second_half)


def first_frames_kernel(
    last_col, previous, begun, time, spatial, spatial_bias, half_done, target, *scratch
):
    del half_done
    first_half, second_half = scratch[:5], scratch[5:]
    whole = time[...].reshape(3 * C, 2 * C)
    first_half[0][...] = begun[0] + dot(
        jnp.concatenate([previous[0], previous[1]], axis=1), whole[: 2 * C]
    )
    second_half[0][...] = begun[1] + dot(previous[1], whole[:C])
    upsampled(last_col, spatial, spatial_bias, target, 0, first_half, second_half)


def parity_weights(weight, phases):
    for start, count in ((0, 128), (128, OUTC - 128)):
        part = slice(start, start + count)
        wide = [[weight[row, col, part, :].astype(F32) for col in range(3)] for row in range(3)]
        for parity_row in range(2):
            for near in range(2):
                first, last = ((0, 0), (1, 2)) if parity_row == 0 else ((0, 1), (2, 2))
                low, high = (first, last)[near]
                taps = wide[low]
                if high > low:
                    taps = [one + other for one, other in zip(wide[low], wide[high])]
                for parity_col in range(2):
                    phase = parity_row * 2 + parity_col
                    if parity_col == 0:
                        pair = [taps[0], taps[1] + taps[2]]
                    else:
                        pair = [taps[0] + taps[1], taps[2]]
                    for index in range(2):
                        block = pair[index]
                        if count < 128:
                            none = jnp.zeros((128 - count, C), F32)
                            block = jnp.concatenate([block, none], axis=0)
                        phases[phase, near, index * C : (index + 1) * C, start : start + 128] = (
                            block.T.astype(BF16)
                        )


def cost(macs, bytes_accessed):
    return pl.CostEstimate(flops=2 * macs, bytes_accessed=bytes_accessed, transcendentals=0)


def call(kernel, name, estimate, limit=LIMIT, **rest):
    return pl.pallas_call(
        kernel,
        name=name,
        cost_estimate=estimate,
        compiler_params=pltpu.CompilerParams(vmem_limit_bytes=limit * 2**20),
        **rest,
    )


def swap_rows(block):
    return lax.ppermute(block, "row", [(0, 1), (1, 0)])


def to_later_frames(block):
    return lax.ppermute(block, "tm", [(i, i + 1) for i in range(lax.axis_size("tm") - 1)])


def across_columns(block):
    count = lax.axis_size("col")
    route = [(i, i - 1) for i in range(1, count)]
    route += [(count + i, count + i + 1) for i in range(count - 1)]
    return lax.ppermute(block, ("row", "col"), route)


def on_device(
    latents, norm_gain, conv_weight, conv_bias, time_weight, time_bias, spatial_weight, spatial_bias
):
    last_col = lax.axis_size("col") - 1
    other = swap_rows(latents)
    own = latents
    spatial_weight = jnp.swapaxes(spatial_weight, 2, 3)
    held = call(
        own_edge_kernel,
        "own_edge",
        cost(2**33, 2**20),
        out_shape=jax.ShapeDtypeStruct((8, 8, C), F32),
        in_specs=[VMEM],
        out_specs=VMEM,
    )(own)
    edge = call(
        edge_kernel,
        "edge",
        cost(2**33, 2**20),
        out_shape=jax.ShapeDtypeStruct((4, 2, 8, C), BF16),
        in_specs=[VMEM] * 2,
        out_specs=VMEM,
        scratch_shapes=[pltpu.VMEM((8, 8, C), F32)],
    )(held, other)
    mine = across_columns(edge)

    inner_shape = jax.ShapeDtypeStruct((MROWS * W, 2 * C), F32)
    inner_patches = pltpu.VMEM((MROWS * W, 9 * C), BF16)
    inner_cost = cost(2 * MROWS * W * 9 * C * C, 7 * 2**20)
    activated, edges, inner3, inner1 = call(
        activate_kernel,
        "activated",
        cost(4 * MROWS * W * 9 * C * C, 7 * 2**20),
        out_shape=(
            jax.ShapeDtypeStruct((4, MROWS + 2, W, C), BF16),
            jax.ShapeDtypeStruct((4, 2, 8, C), F32),
            inner_shape,
            inner_shape,
        ),
        in_specs=[VMEM] * 4,
        out_specs=(VMEM,) * 4,
        scratch_shapes=[inner_patches, inner_patches],
    )(own, other, norm_gain, conv_weight)
    mine, activated = lax.optimization_barrier((mine, activated))
    theirs = swap_rows(mine)
    inner2 = call(
        inner_kernel,
        "inner",
        inner_cost,
        out_shape=inner_shape,
        in_specs=[VMEM] * 2,
        out_specs=VMEM,
        scratch_shapes=[inner_patches],
    )(activated, conv_weight)

    mixed_shape = jax.ShapeDtypeStruct((2, BLOCK, C), BF16)
    onward, crossing, outer = call(
        send_kernel,
        "partial_for_next",
        cost(2 * 96 * 9 * C * C, 10 * 2**20),
        out_shape=(
            mixed_shape,
            jax.ShapeDtypeStruct((2, BLOCK, C), F32),
            jax.ShapeDtypeStruct((4, 4, 8, C), F32),
        ),
        in_specs=[VMEM] * 8,
        out_specs=(VMEM,) * 3,
        scratch_shapes=[pltpu.VMEM((96, 9 * C), BF16), pltpu.VMEM((3, BLOCK, 2 * C), F32)],
    )(edges, mine, theirs, norm_gain, conv_weight, inner1, inner2, inner3)
    onward = to_later_frames(onward)

    frame_patches = pltpu.VMEM((BLOCK, 9 * C), BF16)
    mixed, patches = call(
        own_kernel,
        "mixed_last",
        cost(3 * BLOCK * 9 * C * C, 10 * 2**20),
        out_shape=(mixed_shape, jax.ShapeDtypeStruct((BLOCK, 9 * C), BF16)),
        in_specs=[VMEM] * 10,
        out_specs=(VMEM,) * 2,
        scratch_shapes=[frame_patches, frame_patches],
    )(activated, edges, outer, conv_weight, crossing, own, other, mine, theirs, conv_bias)
    previous = to_later_frames(mixed)

    out_shape = jax.ShapeDtypeStruct((8, 2 * OWN, 2 * W, OUTC), BF16)
    scratch = 2 * [
        pltpu.VMEM((BLOCK, 2 * C), F32),
        pltpu.VMEM((2, OWN + 2, W, 3 * C), BF16),
        pltpu.VMEM((2, 2, 2 * OWN, 2 * W, 128), F32),
        pltpu.VMEM((2, 2 * OWN, 2 * W, OUTC), BF16),
        pltpu.SemaphoreType.DMA((2,)),
    ]
    late_cost = cost(2 * BLOCK * 6 * C * C + 16 * 512 * C * WIDE, 6 * 2**20)

    part, spatial = call(
        first_part_kernel,
        "mixed_first",
        cost(3 * BLOCK * 9 * C * C, 10 * 2**20),
        out_shape=(
            jax.ShapeDtypeStruct((2, BLOCK, C), F32),
            jax.ShapeDtypeStruct((4, 2, 2 * C, WIDE), BF16),
        ),
        in_specs=[VMEM] * 11,
        out_specs=(VMEM,) * 2,
        scratch_shapes=[frame_patches],
    )(
        patches, activated, edges, outer, conv_weight, own, other, mine, theirs, conv_bias,
        spatial_weight,
    )

    def last_frames(*refs):
        last_frames_kernel(last_col, *refs)

    begun, half_done = call(
        last_frames,
        "upsample_last",
        late_cost,
        out_shape=(jax.ShapeDtypeStruct((2, BLOCK, 2 * C), F32), out_shape),
        in_specs=[VMEM] * 7,
        out_specs=(VMEM, HBM),
        scratch_shapes=scratch,
    )(part, onward, mixed, time_weight, time_bias, spatial, spatial_bias)

    def first_frames(*refs):
        first_frames_kernel(last_col, *refs)

    return call(
        first_frames,
        "upsample_first",
        late_cost,
        out_shape=out_shape,
        in_specs=[VMEM] * 5 + [HBM],
        out_specs=HBM,
        scratch_shapes=scratch,
        input_output_aliases={5: 0},
    )(previous, begun, time_weight, spatial, spatial_bias, half_done)


def solution(mesh):
    placed = (P("tm", "row", "col", None), P(), P(), P(), P(), P(), P(), P())
    return jax.shard_map(
        on_device,
        mesh=mesh,
        in_specs=placed,
        out_specs=P("tm", "row", "col", None),
        check_vma=False,
    )
```

```python
import jax
import jax.numpy as jnp
from jax import lax
from jax.experimental import pallas as pl
from jax.experimental.pallas import tpu as pltpu
from jax.sharding import PartitionSpec as P

F32 = jnp.float32
BF16 = jnp.bfloat16
HBM = pl.BlockSpec(memory_space=pltpu.HBM)
VMEM = pl.BlockSpec(memory_space=pltpu.VMEM)

C = 384
OUTC = 192
WIDE = 256
W = 32
OWN = 4
MROWS = 5
SIDE = 16
BLOCK = MROWS * W + SIDE
SENT = OWN * W + SIDE
LIMIT = 24


def activate(values, gain):
    scale = lax.rsqrt(jnp.mean(values * values, axis=-1, keepdims=True) + 1e-06)
    half = values * scale * (0.5 * gain)
    return half + half * jnp.tanh(half)


def dot(left, right):
    return jnp.dot(left, right, preferred_element_type=F32)


def moved_columns(values, left, right):
    place = lax.broadcasted_iota(jnp.int32, values.shape, 0)
    before = jnp.where(place == 0, left, pltpu.roll(values, 1, 0))
    after = jnp.where(place == W - 1, right, pltpu.roll(values, W - 1, 0))
    return before.astype(BF16), values.astype(BF16), after.astype(BF16)


def slot_order(rows, core):
    place = lax.broadcasted_iota(jnp.int32, rows.shape, 0)
    upper = jnp.where(place == 0, 0.0, pltpu.roll(rows, 1, 0))
    lower = jnp.where(place >= 6, 0.0, pltpu.roll(rows, 6, 0))
    return jnp.where(core == 0, upper, lower)


def cut_columns(source, first, core, held):
    start = pl.multiple_of(core * 16, 16)
    for frame in range(4):
        for row in range(OWN):
            values = source[frame, row, pl.ds(start, 16), :].astype(F32)
            values = jnp.where(core == 0, values, pltpu.roll(values, 2, 0))
            for col in range(2):
                held[2 * frame + col, pl.ds(first + row, 1), :] = values[col : col + 1]


def own_edge_kernel(own, held):
    core = lax.axis_index("row")
    cut_columns(own, core * OWN, core, held)


def edge_kernel(held, other, edge, rest):
    core = lax.axis_index("row")
    cut_columns(other, OWN - core * OWN, core, rest)
    place = lax.broadcasted_iota(jnp.int32, (8, C), 0)
    mine = (place < OWN) == (core == 0)
    for frame in range(4):
        for col in range(2):
            index = 2 * frame + col
            edge[frame, col] = jnp.where(mine, held[index], rest[index]).astype(BF16)


def activate_kernel(
    own, other, gain, weight, activated, edges, third, first, second_patches,
    third_patches, first_patches,
):
    core = lax.axis_index("row")
    scale = gain[...].reshape(1, C)
    edges[...] = jnp.zeros(edges.shape, F32)

    def one(frame):
        for slot in range(MROWS + 2):
            if slot == 0:
                values = other[frame, 2].astype(F32) * core.astype(F32)
            elif slot == 1:
                values = jnp.where(core == 0, own[frame, 0], other[frame, 3]).astype(F32)
            elif slot == 5:
                values = jnp.where(core == 0, other[frame, 0], own[frame, 3]).astype(F32)
            elif slot == 6:
                values = other[frame, 1].astype(F32) * (1 - core).astype(F32)
            else:
                values = own[frame, slot - 1 - core].astype(F32)
            values = activate(values, scale)
            edges[frame, 0, slot : slot + 1, :] = values[0:1]
            edges[frame, 1, slot : slot + 1, :] = values[W - 1 : W]
            activated[frame, slot] = values.astype(BF16)

    one(3)
    inner_patches(3, activated, third_patches)
    third[...] = dot(third_patches[...], early_weight(weight))
    one(1)
    inner_patches(1, activated, first_patches)
    first[...] = dot(first_patches[...], early_weight(weight))
    one(2)
    inner_patches(2, activated, second_patches)
    one(0)


def inner_kernel(patches, weight, total):
    total[...] = dot(patches[...], early_weight(weight))


def halo_columns(frame, mine, theirs, core):
    columns = []
    for col in range(4):
        first, second = (theirs, mine) if col < 2 else (mine, theirs)
        rows = jnp.where(core == 0, first[frame, col % 2], second[frame, col % 2]).astype(F32)
        columns.append(slot_order(rows, core))
    return columns


def fill_rows(at, slot, values, left, right, patches):
    moved = moved_columns(values, left, right)
    for tap_row in range(3):
        out_row = slot - tap_row
        if 0 <= out_row < MROWS:
            for tap_col in range(3):
                tap = tap_row * 3 + tap_col
                patches[at + out_row * W : at + (out_row + 1) * W, tap * C : (tap + 1) * C] = moved[
                    tap_col
                ]


def fill_patches(frame, at, activated, edges, outer, patches):
    columns = [outer[frame, index] for index in range(4)]
    for slot in range(MROWS + 2):
        left = outer[frame, 1, slot : slot + 1, :]
        right = outer[frame, 2, slot : slot + 1, :]
        fill_rows(at, slot, activated[frame, slot].astype(F32), left, right, patches)
    fill_sides(at + MROWS * W, frame, edges, columns, patches, False)


def fill_sides(at, frame, edges, columns, patches, inner):
    low = [columns[0], columns[1], edges[frame, 0]]
    high = [edges[frame, 1], columns[2], columns[3]]
    none = jnp.zeros((8, C), F32)
    for tap_row in range(3):
        for tap_col in range(3):
            tap = tap_row * 3 + tap_col
            parts = [low[tap_col], high[tap_col]]
            if inner:
                parts.append(columns[1] if tap_col == 0 else none)
                parts.append(columns[2] if tap_col == 2 else none)
            if tap_row:
                parts = [pltpu.roll(one, 8 - tap_row, 0) for one in parts]
            rows = slice(at, at + 8 * len(parts))
            patches[rows, tap * C : (tap + 1) * C] = jnp.concatenate(parts, axis=0).astype(BF16)


def early_weight(weight):
    return jnp.concatenate([step_weight(weight, 0), step_weight(weight, 1)], axis=1)


def inner_patches(frame, activated, patches):
    for slot in range(MROWS + 2):
        fill_rows(0, slot, activated[frame, slot].astype(F32), 0.0, 0.0, patches)


def step_weight(weight, step):
    return weight[step].reshape(9 * C, C)


def outer_columns(frame, mine, theirs, gain, core):
    return [activate(one, gain) for one in halo_columns(frame, mine, theirs, core)]


def send_kernel(
    edges, mine, theirs, gain, weight, inner1, inner2, inner3, onward, crossing, outer, sides, total
):
    core = lax.axis_index("row")
    scale = gain[...].reshape(1, C)
    for frame in (1, 2, 3):
        columns = outer_columns(frame, mine, theirs, scale, core)
        for index in range(4):
            outer[frame, index] = columns[index]
        fill_sides((frame - 1) * 32, frame, edges, columns, sides, True)
    extra = dot(sides[...], early_weight(weight))
    columns = outer_columns(0, mine, theirs, scale, core)
    for index in range(4):
        outer[0, index] = columns[index]
    for index, inner in enumerate((inner1, inner2, inner3)):
        base = index * 32
        total[index, : MROWS * W] = inner[...]
        total[index, MROWS * W :] = extra[base : base + SIDE]
        for row in range(MROWS):
            for at, side in ((row * W, 16), (row * W + W - 1, 24)):
                line = slice(at, at + 1)
                add = slice(base + side + row, base + side + row + 1)
                total[index, line] = inner[line] + extra[add]
    own = pl.ds(pl.multiple_of(core * W, W), OWN * W)
    outer_rows = slice(MROWS * W, BLOCK)
    for target, source in ((slice(0, OWN * W), own), (slice(OWN * W, SENT), outer_rows)):
        onward[0, target] = (total[1, source, :C] + total[2, source, C:]).astype(BF16)
        onward[1, target] = total[2, source, :C].astype(BF16)
    crossing[0] = total[0, :, C:]
    crossing[1] = total[0, :, :C] + total[1, :, C:]


def base_rows(frame, own, other, mine, theirs, bias, core):
    rows = []
    for out_row in range(MROWS):
        if out_row == 0:
            values = jnp.where(core == 0, own[frame, 0], other[frame, 3])
        elif out_row == OWN:
            values = jnp.where(core == 0, other[frame, 0], own[frame, 3])
        else:
            values = own[frame, out_row - core]
        rows.append(values.astype(F32) + bias)
    columns = halo_columns(frame, mine, theirs, core)
    rows.append(pltpu.roll(columns[1], 7, 0) + bias)
    rows.append(pltpu.roll(columns[2], 7, 0) + bias)
    return jnp.concatenate(rows, axis=0)


def own_kernel(
    activated, edges, outer, weight, crossing, own, other, mine, theirs, bias, mixed, patches,
    third_patches, fourth_patches,
):
    core = lax.axis_index("row")
    shift = bias[...].reshape(1, C)
    fill_patches(3, 0, activated, edges, outer, fourth_patches)
    late = dot(fourth_patches[...], step_weight(weight, 2))
    fill_patches(2, 0, activated, edges, outer, third_patches)
    fourth = base_rows(3, own, other, mine, theirs, shift, core)
    mixed[1] = (fourth + late + crossing[1]).astype(BF16)
    late = dot(third_patches[...], step_weight(weight, 2))
    fill_patches(0, 0, activated, edges, outer, patches)
    third = base_rows(2, own, other, mine, theirs, shift, core)
    early = dot(patches[...], step_weight(weight, 0))
    mixed[0] = (third + late + crossing[0] + early).astype(BF16)


def first_part_kernel(
    patches, activated, edges, outer, weight, own, other, mine, theirs, bias, spatial_weight,
    part, spatial,
    second_patches,
):
    core = lax.axis_index("row")
    shift = bias[...].reshape(1, C)
    both = jnp.concatenate([step_weight(weight, 1), step_weight(weight, 2)], axis=1)
    early = dot(patches[...], both)
    parity_weights(spatial_weight, spatial)
    fill_patches(1, 0, activated, edges, outer, second_patches)
    part[0] = base_rows(0, own, other, mine, theirs, shift, core) + early[:, C:]
    late = dot(second_patches[...], step_weight(weight, 2))
    part[1] = base_rows(1, own, other, mine, theirs, shift, core) + early[:, :C] + late


def frame_step(doubled, last_col, framed):
    core = lax.axis_index("row")
    col = lax.axis_index("col")
    not_first = (col > 0).astype(F32)
    not_last = (col < last_col).astype(F32)
    for half in range(2):
        lanes = slice(half * C, (half + 1) * C)

        def row_of(row):
            return (
                doubled[row * W : (row + 1) * W, lanes],
                doubled[MROWS * W + row : MROWS * W + row + 1, lanes] * not_first,
                doubled[MROWS * W + 8 + row : MROWS * W + 9 + row, lanes] * not_last,
            )

        for slot in range(MROWS + 1):
            if slot == 0:
                parts = [jnp.where(core == 0, 0.0, one) for one in row_of(0)]
            elif slot == MROWS:
                parts = [jnp.where(core == 0, one, 0.0) for one in row_of(MROWS - 1)]
            else:
                pairs = zip(row_of(slot - 1), row_of(slot))
                parts = [jnp.where(core == 0, upper, lower) for upper, lower in pairs]
            moved = moved_columns(*parts)
            for tap in range(3):
                framed[half, slot, :, tap * C : (tap + 1) * C] = moved[tap]


def spatial_step(framed, spatial, bias, woven):
    shift = jnp.concatenate([bias[...].reshape(1, OUTC), jnp.zeros((1, WIDE - OUTC), F32)], axis=1)
    for parity_row in range(2):
        for parity_col in range(2):
            phase = parity_row * 2 + parity_col
            lanes = slice(parity_col * C, (parity_col + 2) * C)
            result = shift
            for near in range(2):
                rows = slice(parity_row + near, parity_row + near + OWN)
                result = result + dot(
                    framed[:, rows, :, lanes].reshape(2 * OWN * W, 2 * C),
                    spatial[phase, near],
                )
            for frame in range(2):
                for row in range(OWN):
                    start = (frame * OWN + row) * W
                    for lane in range(2):
                        woven[
                            lane, frame, 2 * row + parity_row, pl.ds(parity_col, W, stride=2), :
                        ] = result[start : start + W, lane * 128 : lane * 128 + 128]


def weave_step(woven, out, target, frame0, sems):
    copies = []
    for frame in range(2):
        for row in range(2 * OWN):
            out[frame, row, :, :128] = woven[0, frame, row].astype(BF16)
            out[frame, row, :, 128:] = woven[1, frame, row][:, : OUTC - 128].astype(BF16)
        copies.append(
            pltpu.make_async_copy(out.at[frame], target.at[frame0 + frame], sems.at[frame])
        )
        copies[-1].start()
    return copies


def upsampled(last_col, spatial, bias, target, frame0, first, second):
    frame_step(first[0], last_col, first[1])
    spatial_step(first[1], spatial, bias, first[2])
    frame_step(second[0], last_col, second[1])
    spatial_step(second[1], spatial, bias, second[2])
    copies = weave_step(first[2], first[3], target, frame0, first[4])
    copies += weave_step(second[2], second[3], target, frame0 + 2, second[4])
    for copy in copies:
        copy.wait()


def last_frames_kernel(
    last_col, part, onward, near, mixed, time, time_bias, spatial, spatial_bias, begun, target,
    *scratch,
):
    first_half, second_half = scratch[:5], scratch[5:]
    core = lax.axis_index("row")

    def whole_block(frame):
        own = onward[frame, : OWN * W].astype(F32)
        extra = near[frame].astype(F32)
        rows = jnp.where(
            core == 0,
            jnp.concatenate([own, extra], axis=0),
            jnp.concatenate([extra, own], axis=0),
        )
        return jnp.concatenate([rows, onward[frame, OWN * W :].astype(F32)], axis=0)

    first = (part[0] + whole_block(0)).astype(BF16)
    second = (part[1] + whole_block(1)).astype(BF16)
    whole = time[...].reshape(3 * C, 2 * C)
    shift = time_bias[...].reshape(1, 2 * C)
    first_half[0][...] = (
        dot(jnp.concatenate([first, second, mixed[0]], axis=1), whole) + shift
    )
    second_half[0][...] = (
        dot(jnp.concatenate([second, mixed[0], mixed[1]], axis=1), whole) + shift
    )
    begun[0] = dot(first, whole[2 * C :]) + shift
    begun[1] = dot(jnp.concatenate([first, second], axis=1), whole[C:]) + shift
    upsampled(last_col, spatial, spatial_bias, target, 4, first_half, second_half)


def first_frames_kernel(
    last_col, previous, begun, time, spatial, spatial_bias, half_done, target, *scratch
):
    del half_done
    first_half, second_half = scratch[:5], scratch[5:]
    whole = time[...].reshape(3 * C, 2 * C)
    first_half[0][...] = begun[0] + dot(
        jnp.concatenate([previous[0], previous[1]], axis=1), whole[: 2 * C]
    )
    second_half[0][...] = begun[1] + dot(previous[1], whole[:C])
    upsampled(last_col, spatial, spatial_bias, target, 0, first_half, second_half)


def parity_weights(weight, phases):
    for start, count in ((0, 128), (128, OUTC - 128)):
        part = slice(start, start + count)
        wide = [[weight[row, col, part, :].astype(F32) for col in range(3)] for row in range(3)]
        for parity_row in range(2):
            for near in range(2):
                first, last = ((0, 0), (1, 2)) if parity_row == 0 else ((0, 1), (2, 2))
                low, high = (first, last)[near]
                taps = wide[low]
                if high > low:
                    taps = [one + other for one, other in zip(wide[low], wide[high])]
                for parity_col in range(2):
                    phase = parity_row * 2 + parity_col
                    if parity_col == 0:
                        pair = [taps[0], taps[1] + taps[2]]
                    else:
                        pair = [taps[0] + taps[1], taps[2]]
                    for index in range(2):
                        block = pair[index]
                        if count < 128:
                            none = jnp.zeros((128 - count, C), F32)
                            block = jnp.concatenate([block, none], axis=0)
                        phases[phase, near, index * C : (index + 1) * C, start : start + 128] = (
                            block.T.astype(BF16)
                        )


def cost(macs, bytes_accessed):
    return pl.CostEstimate(flops=2 * macs, bytes_accessed=bytes_accessed, transcendentals=0)


def call(kernel, name, estimate, limit=LIMIT, **rest):
    return pl.pallas_call(
        kernel,
        name=name,
        cost_estimate=estimate,
        compiler_params=pltpu.CompilerParams(vmem_limit_bytes=limit * 2**20),
        **rest,
    )


def swap_rows(block):
    return lax.ppermute(block, "row", [(0, 1), (1, 0)])


def to_later_frames(block):
    return lax.ppermute(block, "tm", [(i, i + 1) for i in range(lax.axis_size("tm") - 1)])


def across_columns(block):
    count = lax.axis_size("col")
    route = [(i, i - 1) for i in range(1, count)]
    route += [(count + i, count + i + 1) for i in range(count - 1)]
    return lax.ppermute(block, ("row", "col"), route)


def on_device(
    latents, norm_gain, conv_weight, conv_bias, time_weight, time_bias, spatial_weight, spatial_bias
):
    last_col = lax.axis_size("col") - 1
    other = swap_rows(latents)
    own = latents
    spatial_weight = jnp.swapaxes(spatial_weight, 2, 3)
    held = call(
        own_edge_kernel,
        "own_edge",
        cost(2**33, 2**20),
        out_shape=jax.ShapeDtypeStruct((8, 8, C), F32),
        in_specs=[VMEM],
        out_specs=VMEM,
    )(own)
    edge = call(
        edge_kernel,
        "edge",
        cost(2**33, 2**20),
        out_shape=jax.ShapeDtypeStruct((4, 2, 8, C), BF16),
        in_specs=[VMEM] * 2,
        out_specs=VMEM,
        scratch_shapes=[pltpu.VMEM((8, 8, C), F32)],
    )(held, other)
    mine = across_columns(edge)

    inner_shape = jax.ShapeDtypeStruct((MROWS * W, 2 * C), F32)
    inner_cost = cost(2 * MROWS * W * 9 * C * C, 7 * 2**20)
    activated, edges, inner3, inner1, patches2 = call(
        activate_kernel,
        "activated",
        cost(4 * MROWS * W * 9 * C * C, 7 * 2**20),
        out_shape=(
            jax.ShapeDtypeStruct((4, MROWS + 2, W, C), BF16),
            jax.ShapeDtypeStruct((4, 2, 8, C), F32),
            inner_shape,
            inner_shape,
            jax.ShapeDtypeStruct((MROWS * W, 9 * C), BF16),
        ),
        in_specs=[VMEM] * 4,
        out_specs=(VMEM,) * 5,
        scratch_shapes=2 * [pltpu.VMEM((MROWS * W, 9 * C), BF16)],
    )(own, other, norm_gain, conv_weight)
    mine, activated, patches2 = lax.optimization_barrier((mine, activated, patches2))
    theirs = swap_rows(mine)
    inner2 = call(
        inner_kernel,
        "inner",
        inner_cost,
        out_shape=inner_shape,
        in_specs=[VMEM] * 2,
        out_specs=VMEM,
    )(patches2, conv_weight)

    mixed_shape = jax.ShapeDtypeStruct((2, BLOCK, C), BF16)
    onward, crossing, outer = call(
        send_kernel,
        "partial_for_next",
        cost(2 * 96 * 9 * C * C, 10 * 2**20),
        out_shape=(
            jax.ShapeDtypeStruct((2, SENT, C), BF16),
            jax.ShapeDtypeStruct((2, BLOCK, C), F32),
            jax.ShapeDtypeStruct((4, 4, 8, C), F32),
        ),
        in_specs=[VMEM] * 8,
        out_specs=(VMEM,) * 3,
        scratch_shapes=[pltpu.VMEM((96, 9 * C), BF16), pltpu.VMEM((3, BLOCK, 2 * C), F32)],
    )(edges, mine, theirs, norm_gain, conv_weight, inner1, inner2, inner3)
    onward = to_later_frames(onward)

    frame_patches = pltpu.VMEM((BLOCK, 9 * C), BF16)
    mixed, patches = call(
        own_kernel,
        "mixed_last",
        cost(3 * BLOCK * 9 * C * C, 10 * 2**20),
        out_shape=(mixed_shape, jax.ShapeDtypeStruct((BLOCK, 9 * C), BF16)),
        in_specs=[VMEM] * 10,
        out_specs=(VMEM,) * 2,
        scratch_shapes=[frame_patches, frame_patches],
    )(activated, edges, outer, conv_weight, crossing, own, other, mine, theirs, conv_bias)
    previous = to_later_frames(mixed)

    out_shape = jax.ShapeDtypeStruct((8, 2 * OWN, 2 * W, OUTC), BF16)
    scratch = 2 * [
        pltpu.VMEM((BLOCK, 2 * C), F32),
        pltpu.VMEM((2, OWN + 2, W, 3 * C), BF16),
        pltpu.VMEM((2, 2, 2 * OWN, 2 * W, 128), F32),
        pltpu.VMEM((2, 2 * OWN, 2 * W, OUTC), BF16),
        pltpu.SemaphoreType.DMA((2,)),
    ]
    late_cost = cost(2 * BLOCK * 6 * C * C + 16 * 512 * C * WIDE, 6 * 2**20)

    part, spatial = call(
        first_part_kernel,
        "mixed_first",
        cost(3 * BLOCK * 9 * C * C, 10 * 2**20),
        out_shape=(
            jax.ShapeDtypeStruct((2, BLOCK, C), F32),
            jax.ShapeDtypeStruct((4, 2, 2 * C, WIDE), BF16),
        ),
        in_specs=[VMEM] * 11,
        out_specs=(VMEM,) * 2,
        scratch_shapes=[frame_patches],
    )(
        patches, activated, edges, outer, conv_weight, own, other, mine, theirs, conv_bias,
        spatial_weight,
    )

    onward, part = lax.optimization_barrier((onward, part))
    near = jnp.where(
        lax.axis_index("row") == 0, onward[:, (OWN - 1) * W : OWN * W], onward[:, :W]
    )
    near = swap_rows(near)

    def last_frames(*refs):
        last_frames_kernel(last_col, *refs)

    begun, half_done = call(
        last_frames,
        "upsample_last",
        late_cost,
        out_shape=(jax.ShapeDtypeStruct((2, BLOCK, 2 * C), F32), out_shape),
        in_specs=[VMEM] * 8,
        out_specs=(VMEM, HBM),
        scratch_shapes=scratch,
    )(part, onward, near, mixed, time_weight, time_bias, spatial, spatial_bias)

    def first_frames(*refs):
        first_frames_kernel(last_col, *refs)

    return call(
        first_frames,
        "upsample_first",
        late_cost,
        out_shape=out_shape,
        in_specs=[VMEM] * 5 + [HBM],
        out_specs=HBM,
        scratch_shapes=scratch,
        input_output_aliases={5: 0},
    )(previous, begun, time_weight, spatial, spatial_bias, half_done)


def solution(mesh):
    placed = (P("tm", "row", "col", None), P(), P(), P(), P(), P(), P(), P())
    return jax.shard_map(
        on_device,
        mesh=mesh,
        in_specs=placed,
        out_specs=P("tm", "row", "col", None),
        check_vma=False,
    )
```

```python
import jax
import jax.numpy as jnp
from jax import lax
from jax.experimental import pallas as pl
from jax.experimental.pallas import tpu as pltpu
from jax.sharding import PartitionSpec as P

F32 = jnp.float32
BF16 = jnp.bfloat16
HBM = pl.BlockSpec(memory_space=pltpu.HBM)
VMEM = pl.BlockSpec(memory_space=pltpu.VMEM)

C = 384
OUTC = 192
WIDE = 256
W = 32
OWN = 4
MROWS = 5
SIDE = 16
BLOCK = MROWS * W + SIDE
SENT = OWN * W + SIDE
SPLIT = 4 * C
LIMIT = 24


def activate(values, gain):
    scale = lax.rsqrt(jnp.mean(values * values, axis=-1, keepdims=True) + 1e-06)
    half = values * scale * (0.5 * gain)
    return half + half * jnp.tanh(half)


def dot(left, right):
    return jnp.dot(left, right, preferred_element_type=F32)


def moved_columns(values, left, right):
    place = lax.broadcasted_iota(jnp.int32, values.shape, 0)
    before = jnp.where(place == 0, left, pltpu.roll(values, 1, 0))
    after = jnp.where(place == W - 1, right, pltpu.roll(values, W - 1, 0))
    return before.astype(BF16), values.astype(BF16), after.astype(BF16)


def slot_order(rows, core):
    place = lax.broadcasted_iota(jnp.int32, rows.shape, 0)
    upper = jnp.where(place == 0, 0.0, pltpu.roll(rows, 1, 0))
    lower = jnp.where(place >= 6, 0.0, pltpu.roll(rows, 6, 0))
    return jnp.where(core == 0, upper, lower)


def cut_columns(source, first, core, held):
    start = pl.multiple_of(core * 16, 16)
    for frame in range(4):
        for row in range(OWN):
            values = source[frame, row, pl.ds(start, 16), :].astype(F32)
            values = jnp.where(core == 0, values, pltpu.roll(values, 2, 0))
            for col in range(2):
                held[2 * frame + col, pl.ds(first + row, 1), :] = values[col : col + 1]


def own_edge_kernel(own, held):
    core = lax.axis_index("row")
    cut_columns(own, core * OWN, core, held)


def edge_kernel(held, other, edge, rest):
    core = lax.axis_index("row")
    cut_columns(other, OWN - core * OWN, core, rest)
    place = lax.broadcasted_iota(jnp.int32, (8, C), 0)
    mine = (place < OWN) == (core == 0)
    for frame in range(4):
        for col in range(2):
            index = 2 * frame + col
            edge[frame, col] = jnp.where(mine, held[index], rest[index]).astype(BF16)


def activate_kernel(
    own, other, gain, weight, activated, edges, third, first, zero, second_patches, zero_patches,
    third_patches, first_patches,
):
    core = lax.axis_index("row")
    scale = gain[...].reshape(1, C)
    edges[...] = jnp.zeros(edges.shape, F32)

    def one(frame):
        for slot in range(MROWS + 2):
            if slot == 0:
                values = other[frame, 2].astype(F32) * core.astype(F32)
            elif slot == 1:
                values = jnp.where(core == 0, own[frame, 0], other[frame, 3]).astype(F32)
            elif slot == 5:
                values = jnp.where(core == 0, other[frame, 0], own[frame, 3]).astype(F32)
            elif slot == 6:
                values = other[frame, 1].astype(F32) * (1 - core).astype(F32)
            else:
                values = own[frame, slot - 1 - core].astype(F32)
            values = activate(values, scale)
            edges[frame, 0, slot : slot + 1, :] = values[0:1]
            edges[frame, 1, slot : slot + 1, :] = values[W - 1 : W]
            activated[frame, slot] = values.astype(BF16)

    one(3)
    inner_patches(3, activated, third_patches)
    third[...] = dot(third_patches[...], early_weight(weight))
    one(1)
    inner_patches(1, activated, first_patches)
    first[...] = dot(first_patches[...], early_weight(weight))
    one(0)
    inner_patches(0, activated, zero_patches)
    zero[...] = dot(zero_patches[:, :SPLIT], step_weight(weight, 0)[:SPLIT])
    one(2)
    inner_patches(2, activated, second_patches)


def inner_kernel(patches, weight, total):
    total[...] = dot(patches[...], early_weight(weight))


def halo_columns(frame, mine, theirs, core):
    columns = []
    for col in range(4):
        first, second = (theirs, mine) if col < 2 else (mine, theirs)
        rows = jnp.where(core == 0, first[frame, col % 2], second[frame, col % 2]).astype(F32)
        columns.append(slot_order(rows, core))
    return columns


def fill_rows(at, slot, values, left, right, patches):
    moved = moved_columns(values, left, right)
    for tap_row in range(3):
        out_row = slot - tap_row
        if 0 <= out_row < MROWS:
            for tap_col in range(3):
                tap = tap_row * 3 + tap_col
                patches[at + out_row * W : at + (out_row + 1) * W, tap * C : (tap + 1) * C] = moved[
                    tap_col
                ]


def fill_patches(frame, at, activated, edges, outer, patches):
    columns = [outer[frame, index] for index in range(4)]
    for slot in range(MROWS + 2):
        left = outer[frame, 1, slot : slot + 1, :]
        right = outer[frame, 2, slot : slot + 1, :]
        fill_rows(at, slot, activated[frame, slot].astype(F32), left, right, patches)
    fill_sides(at + MROWS * W, frame, edges, columns, patches, False)


def fill_sides(at, frame, edges, columns, patches, inner):
    low = [columns[0], columns[1], edges[frame, 0]]
    high = [edges[frame, 1], columns[2], columns[3]]
    none = jnp.zeros((8, C), F32)
    for tap_row in range(3):
        for tap_col in range(3):
            tap = tap_row * 3 + tap_col
            parts = [low[tap_col], high[tap_col]]
            if inner:
                parts.append(columns[1] if tap_col == 0 else none)
                parts.append(columns[2] if tap_col == 2 else none)
            if tap_row:
                parts = [pltpu.roll(one, 8 - tap_row, 0) for one in parts]
            rows = slice(at, at + 8 * len(parts))
            patches[rows, tap * C : (tap + 1) * C] = jnp.concatenate(parts, axis=0).astype(BF16)


def early_weight(weight):
    return jnp.concatenate([step_weight(weight, 0), step_weight(weight, 1)], axis=1)


def inner_patches(frame, activated, patches):
    for slot in range(MROWS + 2):
        fill_rows(0, slot, activated[frame, slot].astype(F32), 0.0, 0.0, patches)


def step_weight(weight, step):
    return weight[step].reshape(9 * C, C)


def outer_columns(frame, mine, theirs, gain, core):
    return [activate(one, gain) for one in halo_columns(frame, mine, theirs, core)]


def send_kernel(
    edges, mine, theirs, gain, weight, inner0, inner1, inner2, inner3, onward, crossing, outer,
    sides, total,
):
    core = lax.axis_index("row")
    scale = gain[...].reshape(1, C)
    for frame in range(4):
        columns = outer_columns(frame, mine, theirs, scale, core)
        for index in range(4):
            outer[frame, index] = columns[index]
        fill_sides(frame * 32, frame, edges, columns, sides, True)
    extra = dot(sides[...], early_weight(weight))
    for index, inner in enumerate((inner0, inner1, inner2, inner3)):
        base = index * 32
        lanes = slice(0, inner.shape[1])
        total[index, : MROWS * W, lanes] = inner[...]
        total[index, MROWS * W :, lanes] = extra[base : base + SIDE, lanes]
        for row in range(MROWS):
            for at, side in ((row * W, 16), (row * W + W - 1, 24)):
                line = slice(at, at + 1)
                add = slice(base + side + row, base + side + row + 1)
                total[index, line, lanes] = inner[line] + extra[add, lanes]
    own = pl.ds(pl.multiple_of(core * W, W), OWN * W)
    outer_rows = slice(MROWS * W, BLOCK)
    for target, source in ((slice(0, OWN * W), own), (slice(OWN * W, SENT), outer_rows)):
        onward[0, target] = (total[2, source, :C] + total[3, source, C:]).astype(BF16)
        onward[1, target] = total[3, source, :C].astype(BF16)
    crossing[0] = total[1, :, C:] + total[0, :, :C]
    crossing[1] = total[1, :, :C] + total[2, :, C:]


def base_rows(frame, own, other, mine, theirs, bias, core):
    rows = []
    for out_row in range(MROWS):
        if out_row == 0:
            values = jnp.where(core == 0, own[frame, 0], other[frame, 3])
        elif out_row == OWN:
            values = jnp.where(core == 0, other[frame, 0], own[frame, 3])
        else:
            values = own[frame, out_row - core]
        rows.append(values.astype(F32) + bias)
    columns = halo_columns(frame, mine, theirs, core)
    rows.append(pltpu.roll(columns[1], 7, 0) + bias)
    rows.append(pltpu.roll(columns[2], 7, 0) + bias)
    return jnp.concatenate(rows, axis=0)


def own_kernel(
    zero_patches, activated, edges, outer, weight, crossing, own, other, mine, theirs, bias, mixed,
    third_patches, fourth_patches,
):
    core = lax.axis_index("row")
    shift = bias[...].reshape(1, C)
    fill_patches(3, 0, activated, edges, outer, fourth_patches)
    late = dot(fourth_patches[...], step_weight(weight, 2))
    fill_patches(2, 0, activated, edges, outer, third_patches)
    fourth = base_rows(3, own, other, mine, theirs, shift, core)
    mixed[1] = (fourth + late + crossing[1]).astype(BF16)
    late = dot(third_patches[...], step_weight(weight, 2))
    third = base_rows(2, own, other, mine, theirs, shift, core)
    early = dot(zero_patches[:, SPLIT:], step_weight(weight, 0)[SPLIT:])
    early = jnp.concatenate([early, jnp.zeros((SIDE, C), F32)], axis=0)
    mixed[0] = (third + late + crossing[0] + early).astype(BF16)


def first_part_kernel(
    activated, edges, outer, weight, own, other, mine, theirs, bias, spatial_weight,
    part, spatial,
    patches, second_patches,
):
    core = lax.axis_index("row")
    shift = bias[...].reshape(1, C)
    both = jnp.concatenate([step_weight(weight, 1), step_weight(weight, 2)], axis=1)
    fill_patches(0, 0, activated, edges, outer, patches)
    early = dot(patches[...], both)
    parity_weights(spatial_weight, spatial)
    fill_patches(1, 0, activated, edges, outer, second_patches)
    part[0] = base_rows(0, own, other, mine, theirs, shift, core) + early[:, C:]
    late = dot(second_patches[...], step_weight(weight, 2))
    part[1] = base_rows(1, own, other, mine, theirs, shift, core) + early[:, :C] + late


def frame_step(doubled, last_col, framed):
    core = lax.axis_index("row")
    col = lax.axis_index("col")
    not_first = (col > 0).astype(F32)
    not_last = (col < last_col).astype(F32)
    for half in range(2):
        lanes = slice(half * C, (half + 1) * C)

        def row_of(row):
            return (
                doubled[row * W : (row + 1) * W, lanes],
                doubled[MROWS * W + row : MROWS * W + row + 1, lanes] * not_first,
                doubled[MROWS * W + 8 + row : MROWS * W + 9 + row, lanes] * not_last,
            )

        for slot in range(MROWS + 1):
            if slot == 0:
                parts = [jnp.where(core == 0, 0.0, one) for one in row_of(0)]
            elif slot == MROWS:
                parts = [jnp.where(core == 0, one, 0.0) for one in row_of(MROWS - 1)]
            else:
                pairs = zip(row_of(slot - 1), row_of(slot))
                parts = [jnp.where(core == 0, upper, lower) for upper, lower in pairs]
            moved = moved_columns(*parts)
            for tap in range(3):
                framed[half, slot, :, tap * C : (tap + 1) * C] = moved[tap]


def spatial_step(framed, spatial, bias, woven):
    shift = jnp.concatenate([bias[...].reshape(1, OUTC), jnp.zeros((1, WIDE - OUTC), F32)], axis=1)
    for parity_row in range(2):
        for parity_col in range(2):
            phase = parity_row * 2 + parity_col
            lanes = slice(parity_col * C, (parity_col + 2) * C)
            result = shift
            for near in range(2):
                rows = slice(parity_row + near, parity_row + near + OWN)
                result = result + dot(
                    framed[:, rows, :, lanes].reshape(2 * OWN * W, 2 * C),
                    spatial[phase, near],
                )
            for frame in range(2):
                for row in range(OWN):
                    start = (frame * OWN + row) * W
                    for lane in range(2):
                        woven[
                            lane, frame, 2 * row + parity_row, pl.ds(parity_col, W, stride=2), :
                        ] = result[start : start + W, lane * 128 : lane * 128 + 128]


def weave_step(woven, out, target, frame0, sems):
    copies = []
    for frame in range(2):
        for row in range(2 * OWN):
            out[frame, row, :, :128] = woven[0, frame, row].astype(BF16)
            out[frame, row, :, 128:] = woven[1, frame, row][:, : OUTC - 128].astype(BF16)
        copies.append(
            pltpu.make_async_copy(out.at[frame], target.at[frame0 + frame], sems.at[frame])
        )
        copies[-1].start()
    return copies


def upsampled(last_col, spatial, bias, target, frame0, first, second):
    frame_step(first[0], last_col, first[1])
    spatial_step(first[1], spatial, bias, first[2])
    frame_step(second[0], last_col, second[1])
    spatial_step(second[1], spatial, bias, second[2])
    copies = weave_step(first[2], first[3], target, frame0, first[4])
    copies += weave_step(second[2], second[3], target, frame0 + 2, second[4])
    for copy in copies:
        copy.wait()


def last_frames_kernel(
    last_col, part, onward, near, mixed, time, time_bias, spatial, spatial_bias, begun, target,
    *scratch,
):
    first_half, second_half = scratch[:5], scratch[5:]
    core = lax.axis_index("row")

    def whole_block(frame):
        own = onward[frame, : OWN * W].astype(F32)
        extra = near[frame].astype(F32)
        rows = jnp.where(
            core == 0,
            jnp.concatenate([own, extra], axis=0),
            jnp.concatenate([extra, own], axis=0),
        )
        return jnp.concatenate([rows, onward[frame, OWN * W :].astype(F32)], axis=0)

    first = (part[0] + whole_block(0)).astype(BF16)
    second = (part[1] + whole_block(1)).astype(BF16)
    whole = time[...].reshape(3 * C, 2 * C)
    shift = time_bias[...].reshape(1, 2 * C)
    first_half[0][...] = (
        dot(jnp.concatenate([first, second, mixed[0]], axis=1), whole) + shift
    )
    second_half[0][...] = (
        dot(jnp.concatenate([second, mixed[0], mixed[1]], axis=1), whole) + shift
    )
    begun[0] = dot(first, whole[2 * C :]) + shift
    begun[1] = dot(jnp.concatenate([first, second], axis=1), whole[C:]) + shift
    upsampled(last_col, spatial, spatial_bias, target, 4, first_half, second_half)


def first_frames_kernel(
    last_col, previous, begun, time, spatial, spatial_bias, half_done, target, *scratch
):
    del half_done
    first_half, second_half = scratch[:5], scratch[5:]
    whole = time[...].reshape(3 * C, 2 * C)
    first_half[0][...] = begun[0] + dot(
        jnp.concatenate([previous[0], previous[1]], axis=1), whole[: 2 * C]
    )
    second_half[0][...] = begun[1] + dot(previous[1], whole[:C])
    upsampled(last_col, spatial, spatial_bias, target, 0, first_half, second_half)


def parity_weights(weight, phases):
    for start, count in ((0, 128), (128, OUTC - 128)):
        part = slice(start, start + count)
        wide = [[weight[row, col, part, :].astype(F32) for col in range(3)] for row in range(3)]
        for parity_row in range(2):
            for near in range(2):
                first, last = ((0, 0), (1, 2)) if parity_row == 0 else ((0, 1), (2, 2))
                low, high = (first, last)[near]
                taps = wide[low]
                if high > low:
                    taps = [one + other for one, other in zip(wide[low], wide[high])]
                for parity_col in range(2):
                    phase = parity_row * 2 + parity_col
                    if parity_col == 0:
                        pair = [taps[0], taps[1] + taps[2]]
                    else:
                        pair = [taps[0] + taps[1], taps[2]]
                    for index in range(2):
                        block = pair[index]
                        if count < 128:
                            none = jnp.zeros((128 - count, C), F32)
                            block = jnp.concatenate([block, none], axis=0)
                        phases[phase, near, index * C : (index + 1) * C, start : start + 128] = (
                            block.T.astype(BF16)
                        )


def cost(macs, bytes_accessed):
    return pl.CostEstimate(flops=2 * macs, bytes_accessed=bytes_accessed, transcendentals=0)


def call(kernel, name, estimate, limit=LIMIT, **rest):
    return pl.pallas_call(
        kernel,
        name=name,
        cost_estimate=estimate,
        compiler_params=pltpu.CompilerParams(vmem_limit_bytes=limit * 2**20),
        **rest,
    )


def swap_rows(block):
    return lax.ppermute(block, "row", [(0, 1), (1, 0)])


def to_later_frames(block):
    return lax.ppermute(block, "tm", [(i, i + 1) for i in range(lax.axis_size("tm") - 1)])


def across_columns(block):
    count = lax.axis_size("col")
    route = [(i, i - 1) for i in range(1, count)]
    route += [(count + i, count + i + 1) for i in range(count - 1)]
    return lax.ppermute(block, ("row", "col"), route)


def on_device(
    latents, norm_gain, conv_weight, conv_bias, time_weight, time_bias, spatial_weight, spatial_bias
):
    last_col = lax.axis_size("col") - 1
    other = swap_rows(latents)
    own = latents
    spatial_weight = jnp.swapaxes(spatial_weight, 2, 3)
    held = call(
        own_edge_kernel,
        "own_edge",
        cost(2**33, 2**20),
        out_shape=jax.ShapeDtypeStruct((8, 8, C), F32),
        in_specs=[VMEM],
        out_specs=VMEM,
    )(own)
    edge = call(
        edge_kernel,
        "edge",
        cost(2**33, 2**20),
        out_shape=jax.ShapeDtypeStruct((4, 2, 8, C), BF16),
        in_specs=[VMEM] * 2,
        out_specs=VMEM,
        scratch_shapes=[pltpu.VMEM((8, 8, C), F32)],
    )(held, other)
    mine = across_columns(edge)

    inner_shape = jax.ShapeDtypeStruct((MROWS * W, 2 * C), F32)
    inner_cost = cost(2 * MROWS * W * 9 * C * C, 7 * 2**20)
    activated, edges, inner3, inner1, inner0, patches2, patches0 = call(
        activate_kernel,
        "activated",
        cost(4 * MROWS * W * 9 * C * C, 7 * 2**20),
        out_shape=(
            jax.ShapeDtypeStruct((4, MROWS + 2, W, C), BF16),
            jax.ShapeDtypeStruct((4, 2, 8, C), F32),
            inner_shape,
            inner_shape,
            jax.ShapeDtypeStruct((MROWS * W, C), F32),
            jax.ShapeDtypeStruct((MROWS * W, 9 * C), BF16),
            jax.ShapeDtypeStruct((MROWS * W, 9 * C), BF16),
        ),
        in_specs=[VMEM] * 4,
        out_specs=(VMEM,) * 7,
        scratch_shapes=2 * [pltpu.VMEM((MROWS * W, 9 * C), BF16)],
    )(own, other, norm_gain, conv_weight)
    mine, activated, patches2 = lax.optimization_barrier((mine, activated, patches2))
    theirs = swap_rows(mine)
    inner2 = call(
        inner_kernel,
        "inner",
        inner_cost,
        out_shape=inner_shape,
        in_specs=[VMEM] * 2,
        out_specs=VMEM,
    )(patches2, conv_weight)

    mixed_shape = jax.ShapeDtypeStruct((2, BLOCK, C), BF16)
    onward, crossing, outer = call(
        send_kernel,
        "partial_for_next",
        cost(2 * 96 * 9 * C * C, 10 * 2**20),
        out_shape=(
            jax.ShapeDtypeStruct((2, SENT, C), BF16),
            jax.ShapeDtypeStruct((2, BLOCK, C), F32),
            jax.ShapeDtypeStruct((4, 4, 8, C), F32),
        ),
        in_specs=[VMEM] * 9,
        out_specs=(VMEM,) * 3,
        scratch_shapes=[pltpu.VMEM((128, 9 * C), BF16), pltpu.VMEM((4, BLOCK, 2 * C), F32)],
    )(edges, mine, theirs, norm_gain, conv_weight, inner0, inner1, inner2, inner3)
    onward = to_later_frames(onward)

    frame_patches = pltpu.VMEM((BLOCK, 9 * C), BF16)
    mixed = call(
        own_kernel,
        "mixed_last",
        cost(3 * BLOCK * 9 * C * C, 10 * 2**20),
        out_shape=mixed_shape,
        in_specs=[VMEM] * 11,
        out_specs=VMEM,
        scratch_shapes=[frame_patches, frame_patches],
    )(
        patches0, activated, edges, outer, conv_weight, crossing, own, other, mine, theirs,
        conv_bias,
    )
    previous = to_later_frames(mixed)

    out_shape = jax.ShapeDtypeStruct((8, 2 * OWN, 2 * W, OUTC), BF16)
    scratch = 2 * [
        pltpu.VMEM((BLOCK, 2 * C), F32),
        pltpu.VMEM((2, OWN + 2, W, 3 * C), BF16),
        pltpu.VMEM((2, 2, 2 * OWN, 2 * W, 128), F32),
        pltpu.VMEM((2, 2 * OWN, 2 * W, OUTC), BF16),
        pltpu.SemaphoreType.DMA((2,)),
    ]
    late_cost = cost(2 * BLOCK * 6 * C * C + 16 * 512 * C * WIDE, 6 * 2**20)

    part, spatial = call(
        first_part_kernel,
        "mixed_first",
        cost(3 * BLOCK * 9 * C * C, 10 * 2**20),
        out_shape=(
            jax.ShapeDtypeStruct((2, BLOCK, C), F32),
            jax.ShapeDtypeStruct((4, 2, 2 * C, WIDE), BF16),
        ),
        in_specs=[VMEM] * 10,
        out_specs=(VMEM,) * 2,
        scratch_shapes=[frame_patches, frame_patches],
    )(
        activated, edges, outer, conv_weight, own, other, mine, theirs, conv_bias,
        spatial_weight,
    )

    onward, part = lax.optimization_barrier((onward, part))
    near = jnp.where(
        lax.axis_index("row") == 0, onward[:, (OWN - 1) * W : OWN * W], onward[:, :W]
    )
    near = swap_rows(near)

    def last_frames(*refs):
        last_frames_kernel(last_col, *refs)

    begun, half_done = call(
        last_frames,
        "upsample_last",
        late_cost,
        out_shape=(jax.ShapeDtypeStruct((2, BLOCK, 2 * C), F32), out_shape),
        in_specs=[VMEM] * 8,
        out_specs=(VMEM, HBM),
        scratch_shapes=scratch,
    )(part, onward, near, mixed, time_weight, time_bias, spatial, spatial_bias)

    def first_frames(*refs):
        first_frames_kernel(last_col, *refs)

    return call(
        first_frames,
        "upsample_first",
        late_cost,
        out_shape=out_shape,
        in_specs=[VMEM] * 5 + [HBM],
        out_specs=HBM,
        scratch_shapes=scratch,
        input_output_aliases={5: 0},
    )(previous, begun, time_weight, spatial, spatial_bias, half_done)


def solution(mesh):
    placed = (P("tm", "row", "col", None), P(), P(), P(), P(), P(), P(), P())
    return jax.shard_map(
        on_device,
        mesh=mesh,
        in_specs=placed,
        out_specs=P("tm", "row", "col", None),
        check_vma=False,
    )
```

```python
import jax
import jax.numpy as jnp
from jax import lax
from jax.experimental import pallas as pl
from jax.experimental.pallas import tpu as pltpu
from jax.sharding import PartitionSpec as P

F32 = jnp.float32
BF16 = jnp.bfloat16
HBM = pl.BlockSpec(memory_space=pltpu.HBM)
VMEM = pl.BlockSpec(memory_space=pltpu.VMEM)

C = 384
OUTC = 192
WIDE = 256
W = 32
OWN = 4
MROWS = 5
SIDE = 16
BLOCK = MROWS * W + SIDE
SENT = OWN * W + SIDE
SPLIT = 6 * C
LIMIT = 24


def activate(values, gain):
    scale = lax.rsqrt(jnp.mean(values * values, axis=-1, keepdims=True) + 1e-06)
    half = values * scale * (0.5 * gain)
    return half + half * jnp.tanh(half)


def dot(left, right):
    return jnp.dot(left, right, preferred_element_type=F32)


def moved_columns(values, left, right):
    place = lax.broadcasted_iota(jnp.int32, values.shape, 0)
    before = jnp.where(place == 0, left, pltpu.roll(values, 1, 0))
    after = jnp.where(place == W - 1, right, pltpu.roll(values, W - 1, 0))
    return before.astype(BF16), values.astype(BF16), after.astype(BF16)


def slot_order(rows, core):
    place = lax.broadcasted_iota(jnp.int32, rows.shape, 0)
    upper = jnp.where(place == 0, 0.0, pltpu.roll(rows, 1, 0))
    lower = jnp.where(place >= 6, 0.0, pltpu.roll(rows, 6, 0))
    return jnp.where(core == 0, upper, lower)


def cut_columns(source, first, core, held):
    start = pl.multiple_of(core * 16, 16)
    for frame in range(4):
        for row in range(OWN):
            values = source[frame, row, pl.ds(start, 16), :].astype(F32)
            values = jnp.where(core == 0, values, pltpu.roll(values, 2, 0))
            for col in range(2):
                held[2 * frame + col, pl.ds(first + row, 1), :] = values[col : col + 1]


def own_edge_kernel(own, held):
    core = lax.axis_index("row")
    cut_columns(own, core * OWN, core, held)


def edge_kernel(held, other, edge, rest):
    core = lax.axis_index("row")
    cut_columns(other, OWN - core * OWN, core, rest)
    place = lax.broadcasted_iota(jnp.int32, (8, C), 0)
    mine = (place < OWN) == (core == 0)
    for frame in range(4):
        for col in range(2):
            index = 2 * frame + col
            edge[frame, col] = jnp.where(mine, held[index], rest[index]).astype(BF16)


def activate_kernel(
    own, other, gain, weight, activated, edges, third, first, zero, second_patches, zero_patches,
    third_patches, first_patches,
):
    core = lax.axis_index("row")
    scale = gain[...].reshape(1, C)
    edges[...] = jnp.zeros(edges.shape, F32)

    def one(frame):
        for slot in range(MROWS + 2):
            if slot == 0:
                values = other[frame, 2].astype(F32) * core.astype(F32)
            elif slot == 1:
                values = jnp.where(core == 0, own[frame, 0], other[frame, 3]).astype(F32)
            elif slot == 5:
                values = jnp.where(core == 0, other[frame, 0], own[frame, 3]).astype(F32)
            elif slot == 6:
                values = other[frame, 1].astype(F32) * (1 - core).astype(F32)
            else:
                values = own[frame, slot - 1 - core].astype(F32)
            values = activate(values, scale)
            edges[frame, 0, slot : slot + 1, :] = values[0:1]
            edges[frame, 1, slot : slot + 1, :] = values[W - 1 : W]
            activated[frame, slot] = values.astype(BF16)

    one(3)
    inner_patches(3, activated, third_patches)
    third[...] = dot(third_patches[...], early_weight(weight))
    one(1)
    inner_patches(1, activated, first_patches)
    first[...] = dot(first_patches[...], early_weight(weight))
    one(0)
    inner_patches(0, activated, zero_patches)
    zero[...] = dot(zero_patches[:, :SPLIT], step_weight(weight, 0)[:SPLIT])
    one(2)
    inner_patches(2, activated, second_patches)


def inner_kernel(patches, weight, total):
    total[...] = dot(patches[...], early_weight(weight))


def halo_columns(frame, mine, theirs, core):
    columns = []
    for col in range(4):
        first, second = (theirs, mine) if col < 2 else (mine, theirs)
        rows = jnp.where(core == 0, first[frame, col % 2], second[frame, col % 2]).astype(F32)
        columns.append(slot_order(rows, core))
    return columns


def fill_rows(at, slot, values, left, right, patches):
    moved = moved_columns(values, left, right)
    for tap_row in range(3):
        out_row = slot - tap_row
        if 0 <= out_row < MROWS:
            for tap_col in range(3):
                tap = tap_row * 3 + tap_col
                patches[at + out_row * W : at + (out_row + 1) * W, tap * C : (tap + 1) * C] = moved[
                    tap_col
                ]


def fill_patches(frame, at, activated, edges, outer, patches):
    columns = [outer[frame, index] for index in range(4)]
    for slot in range(MROWS + 2):
        left = outer[frame, 1, slot : slot + 1, :]
        right = outer[frame, 2, slot : slot + 1, :]
        fill_rows(at, slot, activated[frame, slot].astype(F32), left, right, patches)
    fill_sides(at + MROWS * W, frame, edges, columns, patches, False)


def fill_sides(at, frame, edges, columns, patches, inner):
    low = [columns[0], columns[1], edges[frame, 0]]
    high = [edges[frame, 1], columns[2], columns[3]]
    none = jnp.zeros((8, C), F32)
    for tap_row in range(3):
        for tap_col in range(3):
            tap = tap_row * 3 + tap_col
            parts = [low[tap_col], high[tap_col]]
            if inner:
                parts.append(columns[1] if tap_col == 0 else none)
                parts.append(columns[2] if tap_col == 2 else none)
            if tap_row:
                parts = [pltpu.roll(one, 8 - tap_row, 0) for one in parts]
            rows = slice(at, at + 8 * len(parts))
            patches[rows, tap * C : (tap + 1) * C] = jnp.concatenate(parts, axis=0).astype(BF16)


def early_weight(weight):
    return jnp.concatenate([step_weight(weight, 0), step_weight(weight, 1)], axis=1)


def inner_patches(frame, activated, patches):
    for slot in range(MROWS + 2):
        fill_rows(0, slot, activated[frame, slot].astype(F32), 0.0, 0.0, patches)


def step_weight(weight, step):
    return weight[step].reshape(9 * C, C)


def outer_columns(frame, mine, theirs, gain, core):
    return [activate(one, gain) for one in halo_columns(frame, mine, theirs, core)]


def send_kernel(
    edges, mine, theirs, gain, weight, inner0, inner1, inner2, inner3, onward, crossing, outer,
    sides, total,
):
    core = lax.axis_index("row")
    scale = gain[...].reshape(1, C)
    for frame in range(4):
        columns = outer_columns(frame, mine, theirs, scale, core)
        for index in range(4):
            outer[frame, index] = columns[index]
        fill_sides(frame * 32, frame, edges, columns, sides, True)
    extra = dot(sides[...], early_weight(weight))
    for index, inner in enumerate((inner0, inner1, inner2, inner3)):
        base = index * 32
        lanes = slice(0, inner.shape[1])
        total[index, : MROWS * W, lanes] = inner[...]
        total[index, MROWS * W :, lanes] = extra[base : base + SIDE, lanes]
        for row in range(MROWS):
            for at, side in ((row * W, 16), (row * W + W - 1, 24)):
                line = slice(at, at + 1)
                add = slice(base + side + row, base + side + row + 1)
                total[index, line, lanes] = inner[line] + extra[add, lanes]
    own = pl.ds(pl.multiple_of(core * W, W), OWN * W)
    outer_rows = slice(MROWS * W, BLOCK)
    for target, source in ((slice(0, OWN * W), own), (slice(OWN * W, SENT), outer_rows)):
        onward[0, target] = (total[2, source, :C] + total[3, source, C:]).astype(BF16)
        onward[1, target] = total[3, source, :C].astype(BF16)
    crossing[0] = total[1, :, C:] + total[0, :, :C]
    crossing[1] = total[1, :, :C] + total[2, :, C:]


def base_rows(frame, own, other, mine, theirs, bias, core):
    rows = []
    for out_row in range(MROWS):
        if out_row == 0:
            values = jnp.where(core == 0, own[frame, 0], other[frame, 3])
        elif out_row == OWN:
            values = jnp.where(core == 0, other[frame, 0], own[frame, 3])
        else:
            values = own[frame, out_row - core]
        rows.append(values.astype(F32) + bias)
    columns = halo_columns(frame, mine, theirs, core)
    rows.append(pltpu.roll(columns[1], 7, 0) + bias)
    rows.append(pltpu.roll(columns[2], 7, 0) + bias)
    return jnp.concatenate(rows, axis=0)


def own_kernel(
    zero_patches, activated, edges, outer, weight, crossing, own, other, mine, theirs, bias, mixed,
    third_patches, fourth_patches,
):
    core = lax.axis_index("row")
    shift = bias[...].reshape(1, C)
    fill_patches(3, 0, activated, edges, outer, fourth_patches)
    late = dot(fourth_patches[...], step_weight(weight, 2))
    fill_patches(2, 0, activated, edges, outer, third_patches)
    fourth = base_rows(3, own, other, mine, theirs, shift, core)
    mixed[1] = (fourth + late + crossing[1]).astype(BF16)
    late = dot(third_patches[...], step_weight(weight, 2))
    third = base_rows(2, own, other, mine, theirs, shift, core)
    early = dot(zero_patches[:, SPLIT:], step_weight(weight, 0)[SPLIT:])
    early = jnp.concatenate([early, jnp.zeros((SIDE, C), F32)], axis=0)
    mixed[0] = (third + late + crossing[0] + early).astype(BF16)


def first_part_kernel(
    activated, edges, outer, weight, own, other, mine, theirs, bias, spatial_weight,
    part, spatial,
    patches, second_patches,
):
    core = lax.axis_index("row")
    shift = bias[...].reshape(1, C)
    both = jnp.concatenate([step_weight(weight, 1), step_weight(weight, 2)], axis=1)
    fill_patches(0, 0, activated, edges, outer, patches)
    early = dot(patches[...], both)
    parity_weights(spatial_weight, spatial)
    fill_patches(1, 0, activated, edges, outer, second_patches)
    part[0] = base_rows(0, own, other, mine, theirs, shift, core) + early[:, C:]
    late = dot(second_patches[...], step_weight(weight, 2))
    part[1] = base_rows(1, own, other, mine, theirs, shift, core) + early[:, :C] + late


def frame_step(doubled, last_col, framed):
    core = lax.axis_index("row")
    col = lax.axis_index("col")
    not_first = (col > 0).astype(F32)
    not_last = (col < last_col).astype(F32)
    for half in range(2):
        lanes = slice(half * C, (half + 1) * C)

        def row_of(row):
            return (
                doubled[row * W : (row + 1) * W, lanes],
                doubled[MROWS * W + row : MROWS * W + row + 1, lanes] * not_first,
                doubled[MROWS * W + 8 + row : MROWS * W + 9 + row, lanes] * not_last,
            )

        for slot in range(MROWS + 1):
            if slot == 0:
                parts = [jnp.where(core == 0, 0.0, one) for one in row_of(0)]
            elif slot == MROWS:
                parts = [jnp.where(core == 0, one, 0.0) for one in row_of(MROWS - 1)]
            else:
                pairs = zip(row_of(slot - 1), row_of(slot))
                parts = [jnp.where(core == 0, upper, lower) for upper, lower in pairs]
            moved = moved_columns(*parts)
            for tap in range(3):
                framed[half, slot, :, tap * C : (tap + 1) * C] = moved[tap]


def spatial_step(framed, spatial, bias, woven):
    shift = jnp.concatenate([bias[...].reshape(1, OUTC), jnp.zeros((1, WIDE - OUTC), F32)], axis=1)
    for parity_row in range(2):
        for parity_col in range(2):
            phase = parity_row * 2 + parity_col
            lanes = slice(parity_col * C, (parity_col + 2) * C)
            result = shift
            for near in range(2):
                rows = slice(parity_row + near, parity_row + near + OWN)
                result = result + dot(
                    framed[:, rows, :, lanes].reshape(2 * OWN * W, 2 * C),
                    spatial[phase, near],
                )
            for frame in range(2):
                for row in range(OWN):
                    start = (frame * OWN + row) * W
                    for lane in range(2):
                        woven[
                            lane, frame, 2 * row + parity_row, pl.ds(parity_col, W, stride=2), :
                        ] = result[start : start + W, lane * 128 : lane * 128 + 128]


def weave_step(woven, out, target, frame0, sems):
    copies = []
    for frame in range(2):
        for row in range(2 * OWN):
            out[frame, row, :, :128] = woven[0, frame, row].astype(BF16)
            out[frame, row, :, 128:] = woven[1, frame, row][:, : OUTC - 128].astype(BF16)
        copies.append(
            pltpu.make_async_copy(out.at[frame], target.at[frame0 + frame], sems.at[frame])
        )
        copies[-1].start()
    return copies


def upsampled(last_col, spatial, bias, target, frame0, first, second):
    frame_step(first[0], last_col, first[1])
    spatial_step(first[1], spatial, bias, first[2])
    frame_step(second[0], last_col, second[1])
    spatial_step(second[1], spatial, bias, second[2])
    copies = weave_step(first[2], first[3], target, frame0, first[4])
    copies += weave_step(second[2], second[3], target, frame0 + 2, second[4])
    for copy in copies:
        copy.wait()


def last_frames_kernel(
    last_col, part, onward, near, mixed, time, time_bias, spatial, spatial_bias, begun, target,
    *scratch,
):
    first_half, second_half = scratch[:5], scratch[5:]
    core = lax.axis_index("row")

    def whole_block(frame):
        own = onward[frame, : OWN * W].astype(F32)
        extra = near[frame].astype(F32)
        rows = jnp.where(
            core == 0,
            jnp.concatenate([own, extra], axis=0),
            jnp.concatenate([extra, own], axis=0),
        )
        return jnp.concatenate([rows, onward[frame, OWN * W :].astype(F32)], axis=0)

    first = (part[0] + whole_block(0)).astype(BF16)
    second = (part[1] + whole_block(1)).astype(BF16)
    whole = time[...].reshape(3 * C, 2 * C)
    shift = time_bias[...].reshape(1, 2 * C)
    first_half[0][...] = (
        dot(jnp.concatenate([first, second, mixed[0]], axis=1), whole) + shift
    )
    second_half[0][...] = (
        dot(jnp.concatenate([second, mixed[0], mixed[1]], axis=1), whole) + shift
    )
    begun[0] = dot(first, whole[2 * C :]) + shift
    begun[1] = dot(jnp.concatenate([first, second], axis=1), whole[C:]) + shift
    upsampled(last_col, spatial, spatial_bias, target, 4, first_half, second_half)


def first_frames_kernel(
    last_col, previous, begun, time, spatial, spatial_bias, half_done, target, *scratch
):
    del half_done
    first_half, second_half = scratch[:5], scratch[5:]
    whole = time[...].reshape(3 * C, 2 * C)
    first_half[0][...] = begun[0] + dot(
        jnp.concatenate([previous[0], previous[1]], axis=1), whole[: 2 * C]
    )
    second_half[0][...] = begun[1] + dot(previous[1], whole[:C])
    upsampled(last_col, spatial, spatial_bias, target, 0, first_half, second_half)


def parity_weights(weight, phases):
    for start, count in ((0, 128), (128, OUTC - 128)):
        part = slice(start, start + count)
        wide = [[weight[row, col, part, :].astype(F32) for col in range(3)] for row in range(3)]
        for parity_row in range(2):
            for near in range(2):
                first, last = ((0, 0), (1, 2)) if parity_row == 0 else ((0, 1), (2, 2))
                low, high = (first, last)[near]
                taps = wide[low]
                if high > low:
                    taps = [one + other for one, other in zip(wide[low], wide[high])]
                for parity_col in range(2):
                    phase = parity_row * 2 + parity_col
                    if parity_col == 0:
                        pair = [taps[0], taps[1] + taps[2]]
                    else:
                        pair = [taps[0] + taps[1], taps[2]]
                    for index in range(2):
                        block = pair[index]
                        if count < 128:
                            none = jnp.zeros((128 - count, C), F32)
                            block = jnp.concatenate([block, none], axis=0)
                        phases[phase, near, index * C : (index + 1) * C, start : start + 128] = (
                            block.T.astype(BF16)
                        )


def cost(macs, bytes_accessed):
    return pl.CostEstimate(flops=2 * macs, bytes_accessed=bytes_accessed, transcendentals=0)


def call(kernel, name, estimate, limit=LIMIT, **rest):
    return pl.pallas_call(
        kernel,
        name=name,
        cost_estimate=estimate,
        compiler_params=pltpu.CompilerParams(vmem_limit_bytes=limit * 2**20),
        **rest,
    )


def swap_rows(block):
    return lax.ppermute(block, "row", [(0, 1), (1, 0)])


def to_later_frames(block):
    return lax.ppermute(block, "tm", [(i, i + 1) for i in range(lax.axis_size("tm") - 1)])


def across_columns(block):
    count = lax.axis_size("col")
    route = [(i, i - 1) for i in range(1, count)]
    route += [(count + i, count + i + 1) for i in range(count - 1)]
    return lax.ppermute(block, ("row", "col"), route)


def on_device(
    latents, norm_gain, conv_weight, conv_bias, time_weight, time_bias, spatial_weight, spatial_bias
):
    last_col = lax.axis_size("col") - 1
    other = swap_rows(latents)
    own = latents
    spatial_weight = jnp.swapaxes(spatial_weight, 2, 3)
    held = call(
        own_edge_kernel,
        "own_edge",
        cost(2**33, 2**20),
        out_shape=jax.ShapeDtypeStruct((8, 8, C), F32),
        in_specs=[VMEM],
        out_specs=VMEM,
    )(own)
    edge = call(
        edge_kernel,
        "edge",
        cost(2**33, 2**20),
        out_shape=jax.ShapeDtypeStruct((4, 2, 8, C), BF16),
        in_specs=[VMEM] * 2,
        out_specs=VMEM,
        scratch_shapes=[pltpu.VMEM((8, 8, C), F32)],
    )(held, other)
    mine = across_columns(edge)

    inner_shape = jax.ShapeDtypeStruct((MROWS * W, 2 * C), F32)
    inner_cost = cost(2 * MROWS * W * 9 * C * C, 7 * 2**20)
    activated, edges, inner3, inner1, inner0, patches2, patches0 = call(
        activate_kernel,
        "activated",
        cost(4 * MROWS * W * 9 * C * C, 7 * 2**20),
        out_shape=(
            jax.ShapeDtypeStruct((4, MROWS + 2, W, C), BF16),
            jax.ShapeDtypeStruct((4, 2, 8, C), F32),
            inner_shape,
            inner_shape,
            jax.ShapeDtypeStruct((MROWS * W, C), F32),
            jax.ShapeDtypeStruct((MROWS * W, 9 * C), BF16),
            jax.ShapeDtypeStruct((MROWS * W, 9 * C), BF16),
        ),
        in_specs=[VMEM] * 4,
        out_specs=(VMEM,) * 7,
        scratch_shapes=2 * [pltpu.VMEM((MROWS * W, 9 * C), BF16)],
    )(own, other, norm_gain, conv_weight)
    mine, activated, patches2 = lax.optimization_barrier((mine, activated, patches2))
    theirs = swap_rows(mine)
    inner2 = call(
        inner_kernel,
        "inner",
        inner_cost,
        out_shape=inner_shape,
        in_specs=[VMEM] * 2,
        out_specs=VMEM,
    )(patches2, conv_weight)

    mixed_shape = jax.ShapeDtypeStruct((2, BLOCK, C), BF16)
    onward, crossing, outer = call(
        send_kernel,
        "partial_for_next",
        cost(2 * 96 * 9 * C * C, 10 * 2**20),
        out_shape=(
            jax.ShapeDtypeStruct((2, SENT, C), BF16),
            jax.ShapeDtypeStruct((2, BLOCK, C), F32),
            jax.ShapeDtypeStruct((4, 4, 8, C), F32),
        ),
        in_specs=[VMEM] * 9,
        out_specs=(VMEM,) * 3,
        scratch_shapes=[pltpu.VMEM((128, 9 * C), BF16), pltpu.VMEM((4, BLOCK, 2 * C), F32)],
    )(edges, mine, theirs, norm_gain, conv_weight, inner0, inner1, inner2, inner3)
    onward = to_later_frames(onward)

    frame_patches = pltpu.VMEM((BLOCK, 9 * C), BF16)
    mixed = call(
        own_kernel,
        "mixed_last",
        cost(3 * BLOCK * 9 * C * C, 10 * 2**20),
        out_shape=mixed_shape,
        in_specs=[VMEM] * 11,
        out_specs=VMEM,
        scratch_shapes=[frame_patches, frame_patches],
    )(
        patches0, activated, edges, outer, conv_weight, crossing, own, other, mine, theirs,
        conv_bias,
    )
    previous = to_later_frames(mixed)

    out_shape = jax.ShapeDtypeStruct((8, 2 * OWN, 2 * W, OUTC), BF16)
    scratch = 2 * [
        pltpu.VMEM((BLOCK, 2 * C), F32),
        pltpu.VMEM((2, OWN + 2, W, 3 * C), BF16),
        pltpu.VMEM((2, 2, 2 * OWN, 2 * W, 128), F32),
        pltpu.VMEM((2, 2 * OWN, 2 * W, OUTC), BF16),
        pltpu.SemaphoreType.DMA((2,)),
    ]
    late_cost = cost(2 * BLOCK * 6 * C * C + 16 * 512 * C * WIDE, 6 * 2**20)

    part, spatial = call(
        first_part_kernel,
        "mixed_first",
        cost(3 * BLOCK * 9 * C * C, 10 * 2**20),
        out_shape=(
            jax.ShapeDtypeStruct((2, BLOCK, C), F32),
            jax.ShapeDtypeStruct((4, 2, 2 * C, WIDE), BF16),
        ),
        in_specs=[VMEM] * 10,
        out_specs=(VMEM,) * 2,
        scratch_shapes=[frame_patches, frame_patches],
    )(
        activated, edges, outer, conv_weight, own, other, mine, theirs, conv_bias,
        spatial_weight,
    )

    onward, part = lax.optimization_barrier((onward, part))
    near = jnp.where(
        lax.axis_index("row") == 0, onward[:, (OWN - 1) * W : OWN * W], onward[:, :W]
    )
    near = swap_rows(near)

    def last_frames(*refs):
        last_frames_kernel(last_col, *refs)

    begun, half_done = call(
        last_frames,
        "upsample_last",
        late_cost,
        out_shape=(jax.ShapeDtypeStruct((2, BLOCK, 2 * C), F32), out_shape),
        in_specs=[VMEM] * 8,
        out_specs=(VMEM, HBM),
        scratch_shapes=scratch,
    )(part, onward, near, mixed, time_weight, time_bias, spatial, spatial_bias)

    def first_frames(*refs):
        first_frames_kernel(last_col, *refs)

    return call(
        first_frames,
        "upsample_first",
        late_cost,
        out_shape=out_shape,
        in_specs=[VMEM] * 5 + [HBM],
        out_specs=HBM,
        scratch_shapes=scratch,
        input_output_aliases={5: 0},
    )(previous, begun, time_weight, spatial, spatial_bias, half_done)


def solution(mesh):
    placed = (P("tm", "row", "col", None), P(), P(), P(), P(), P(), P(), P())
    return jax.shard_map(
        on_device,
        mesh=mesh,
        in_specs=placed,
        out_specs=P("tm", "row", "col", None),
        check_vma=False,
    )
```

```python
import jax
import jax.numpy as jnp
from jax import lax
from jax.experimental import pallas as pl
from jax.experimental.pallas import tpu as pltpu
from jax.sharding import PartitionSpec as P

F32 = jnp.float32
BF16 = jnp.bfloat16
HBM = pl.BlockSpec(memory_space=pltpu.HBM)
VMEM = pl.BlockSpec(memory_space=pltpu.VMEM)

C = 384
OUTC = 192
WIDE = 256
W = 32
OWN = 4
MROWS = 5
SIDE = 16
BLOCK = MROWS * W + SIDE
SENT = OWN * W + SIDE
SPLIT = 4 * C
LIMIT = 24


def activate(values, gain):
    scale = lax.rsqrt(jnp.mean(values * values, axis=-1, keepdims=True) + 1e-06)
    half = values * scale * (0.5 * gain)
    return half + half * jnp.tanh(half)


def dot(left, right):
    return jnp.dot(left, right, preferred_element_type=F32)


def moved_columns(values, left, right):
    place = lax.broadcasted_iota(jnp.int32, values.shape, 0)
    before = jnp.where(place == 0, left, pltpu.roll(values, 1, 0))
    after = jnp.where(place == W - 1, right, pltpu.roll(values, W - 1, 0))
    return before.astype(BF16), values.astype(BF16), after.astype(BF16)


def slot_order(rows, core):
    place = lax.broadcasted_iota(jnp.int32, rows.shape, 0)
    upper = jnp.where(place == 0, 0.0, pltpu.roll(rows, 1, 0))
    lower = jnp.where(place >= 6, 0.0, pltpu.roll(rows, 6, 0))
    return jnp.where(core == 0, upper, lower)


def cut_columns(source, first, core, held):
    start = pl.multiple_of(core * 16, 16)
    for frame in range(4):
        for row in range(OWN):
            values = source[frame, row, pl.ds(start, 16), :].astype(F32)
            values = jnp.where(core == 0, values, pltpu.roll(values, 2, 0))
            for col in range(2):
                held[2 * frame + col, pl.ds(first + row, 1), :] = values[col : col + 1]


def own_edge_kernel(own, held):
    core = lax.axis_index("row")
    cut_columns(own, core * OWN, core, held)


def edge_kernel(held, other, edge, rest):
    core = lax.axis_index("row")
    cut_columns(other, OWN - core * OWN, core, rest)
    place = lax.broadcasted_iota(jnp.int32, (8, C), 0)
    mine = (place < OWN) == (core == 0)
    for frame in range(4):
        for col in range(2):
            index = 2 * frame + col
            edge[frame, col] = jnp.where(mine, held[index], rest[index]).astype(BF16)


def activate_kernel(
    own, other, gain, weight, activated, edges, third, first, zero, second_patches, zero_patches,
    third_patches, first_patches,
):
    core = lax.axis_index("row")
    scale = gain[...].reshape(1, C)
    edges[...] = jnp.zeros(edges.shape, F32)

    def one(frame):
        for slot in range(MROWS + 2):
            if slot == 0:
                values = other[frame, 2].astype(F32) * core.astype(F32)
            elif slot == 1:
                values = jnp.where(core == 0, own[frame, 0], other[frame, 3]).astype(F32)
            elif slot == 5:
                values = jnp.where(core == 0, other[frame, 0], own[frame, 3]).astype(F32)
            elif slot == 6:
                values = other[frame, 1].astype(F32) * (1 - core).astype(F32)
            else:
                values = own[frame, slot - 1 - core].astype(F32)
            values = activate(values, scale)
            edges[frame, 0, slot : slot + 1, :] = values[0:1]
            edges[frame, 1, slot : slot + 1, :] = values[W - 1 : W]
            activated[frame, slot] = values.astype(BF16)

    one(3)
    inner_patches(3, activated, third_patches)
    third[...] = dot(third_patches[...], early_weight(weight))
    one(1)
    inner_patches(1, activated, first_patches)
    first[...] = dot(first_patches[...], early_weight(weight))
    one(0)
    inner_patches(0, activated, zero_patches)
    zero[...] = dot(zero_patches[:, :SPLIT], step_weight(weight, 0)[:SPLIT])
    one(2)
    inner_patches(2, activated, second_patches)


def inner_kernel(patches, weight, total):
    total[...] = dot(patches[...], early_weight(weight))


def halo_columns(frame, mine, theirs, core):
    columns = []
    for col in range(4):
        first, second = (theirs, mine) if col < 2 else (mine, theirs)
        rows = jnp.where(core == 0, first[frame, col % 2], second[frame, col % 2]).astype(F32)
        columns.append(slot_order(rows, core))
    return columns


def fill_rows(at, slot, values, left, right, patches):
    moved = moved_columns(values, left, right)
    for tap_row in range(3):
        out_row = slot - tap_row
        if 0 <= out_row < MROWS:
            for tap_col in range(3):
                tap = tap_row * 3 + tap_col
                patches[at + out_row * W : at + (out_row + 1) * W, tap * C : (tap + 1) * C] = moved[
                    tap_col
                ]


def fill_patches(frame, at, activated, edges, outer, patches):
    columns = [outer[frame, index] for index in range(4)]
    for slot in range(MROWS + 2):
        left = outer[frame, 1, slot : slot + 1, :]
        right = outer[frame, 2, slot : slot + 1, :]
        fill_rows(at, slot, activated[frame, slot].astype(F32), left, right, patches)
    fill_sides(at + MROWS * W, frame, edges, columns, patches, False)


def fill_sides(at, frame, edges, columns, patches, inner):
    low = [columns[0], columns[1], edges[frame, 0]]
    high = [edges[frame, 1], columns[2], columns[3]]
    none = jnp.zeros((8, C), F32)
    for tap_row in range(3):
        for tap_col in range(3):
            tap = tap_row * 3 + tap_col
            parts = [low[tap_col], high[tap_col]]
            if inner:
                parts.append(columns[1] if tap_col == 0 else none)
                parts.append(columns[2] if tap_col == 2 else none)
            if tap_row:
                parts = [pltpu.roll(one, 8 - tap_row, 0) for one in parts]
            rows = slice(at, at + 8 * len(parts))
            patches[rows, tap * C : (tap + 1) * C] = jnp.concatenate(parts, axis=0).astype(BF16)


def early_weight(weight):
    return jnp.concatenate([step_weight(weight, 0), step_weight(weight, 1)], axis=1)


def inner_patches(frame, activated, patches):
    for slot in range(MROWS + 2):
        fill_rows(0, slot, activated[frame, slot].astype(F32), 0.0, 0.0, patches)


def step_weight(weight, step):
    return weight[step].reshape(9 * C, C)


def outer_columns(frame, mine, theirs, gain, core):
    return [activate(one, gain) for one in halo_columns(frame, mine, theirs, core)]


def send_kernel(
    edges, mine, theirs, gain, weight, inner0, inner1, inner2, inner3, onward, crossing, outer,
    sides, total,
):
    core = lax.axis_index("row")
    scale = gain[...].reshape(1, C)
    for frame in range(4):
        columns = outer_columns(frame, mine, theirs, scale, core)
        for index in range(4):
            outer[frame, index] = columns[index]
        fill_sides(frame * 32, frame, edges, columns, sides, True)
    extra = dot(sides[...], early_weight(weight))
    for index, inner in enumerate((inner0, inner1, inner2, inner3)):
        base = index * 32
        lanes = slice(0, inner.shape[1])
        total[index, : MROWS * W, lanes] = inner[...]
        total[index, MROWS * W :, lanes] = extra[base : base + SIDE, lanes]
        for row in range(MROWS):
            for at, side in ((row * W, 16), (row * W + W - 1, 24)):
                line = slice(at, at + 1)
                add = slice(base + side + row, base + side + row + 1)
                total[index, line, lanes] = inner[line] + extra[add, lanes]
    own = pl.ds(pl.multiple_of(core * W, W), OWN * W)
    outer_rows = slice(MROWS * W, BLOCK)
    for target, source in ((slice(0, OWN * W), own), (slice(OWN * W, SENT), outer_rows)):
        onward[0, target] = (total[2, source, :C] + total[3, source, C:]).astype(BF16)
        onward[1, target] = total[3, source, :C].astype(BF16)
    crossing[0] = total[1, :, C:] + total[0, :, :C]
    crossing[1] = total[1, :, :C] + total[2, :, C:]


def base_rows(frame, own, other, mine, theirs, bias, core):
    rows = []
    for out_row in range(MROWS):
        if out_row == 0:
            values = jnp.where(core == 0, own[frame, 0], other[frame, 3])
        elif out_row == OWN:
            values = jnp.where(core == 0, other[frame, 0], own[frame, 3])
        else:
            values = own[frame, out_row - core]
        rows.append(values.astype(F32) + bias)
    columns = halo_columns(frame, mine, theirs, core)
    rows.append(pltpu.roll(columns[1], 7, 0) + bias)
    rows.append(pltpu.roll(columns[2], 7, 0) + bias)
    return jnp.concatenate(rows, axis=0)


def own_kernel(
    zero_patches, activated, edges, outer, weight, crossing, own, other, mine, theirs, bias, mixed,
    third_patches, fourth_patches,
):
    core = lax.axis_index("row")
    shift = bias[...].reshape(1, C)
    early = dot(zero_patches[:, SPLIT:], step_weight(weight, 0)[SPLIT:])
    fill_patches(3, 0, activated, edges, outer, fourth_patches)
    late = dot(fourth_patches[...], step_weight(weight, 2))
    fill_patches(2, 0, activated, edges, outer, third_patches)
    fourth = base_rows(3, own, other, mine, theirs, shift, core)
    mixed[1] = (fourth + late + crossing[1]).astype(BF16)
    late = dot(third_patches[...], step_weight(weight, 2))
    third = base_rows(2, own, other, mine, theirs, shift, core)
    early = jnp.concatenate([early, jnp.zeros((SIDE, C), F32)], axis=0)
    mixed[0] = (third + late + crossing[0] + early).astype(BF16)


def first_part_kernel(
    activated, edges, outer, weight, own, other, mine, theirs, bias, spatial_weight,
    part, spatial,
    patches, second_patches,
):
    core = lax.axis_index("row")
    shift = bias[...].reshape(1, C)
    both = jnp.concatenate([step_weight(weight, 1), step_weight(weight, 2)], axis=1)
    fill_patches(0, 0, activated, edges, outer, patches)
    early = dot(patches[...], both)
    parity_weights(spatial_weight, spatial)
    fill_patches(1, 0, activated, edges, outer, second_patches)
    part[0] = base_rows(0, own, other, mine, theirs, shift, core) + early[:, C:]
    late = dot(second_patches[...], step_weight(weight, 2))
    part[1] = base_rows(1, own, other, mine, theirs, shift, core) + early[:, :C] + late


def frame_step(doubled, last_col, framed):
    core = lax.axis_index("row")
    col = lax.axis_index("col")
    not_first = (col > 0).astype(F32)
    not_last = (col < last_col).astype(F32)
    for half in range(2):
        lanes = slice(half * C, (half + 1) * C)

        def row_of(row):
            return (
                doubled[row * W : (row + 1) * W, lanes],
                doubled[MROWS * W + row : MROWS * W + row + 1, lanes] * not_first,
                doubled[MROWS * W + 8 + row : MROWS * W + 9 + row, lanes] * not_last,
            )

        for slot in range(MROWS + 1):
            if slot == 0:
                parts = [jnp.where(core == 0, 0.0, one) for one in row_of(0)]
            elif slot == MROWS:
                parts = [jnp.where(core == 0, one, 0.0) for one in row_of(MROWS - 1)]
            else:
                pairs = zip(row_of(slot - 1), row_of(slot))
                parts = [jnp.where(core == 0, upper, lower) for upper, lower in pairs]
            moved = moved_columns(*parts)
            for tap in range(3):
                framed[half, slot, :, tap * C : (tap + 1) * C] = moved[tap]


def spatial_step(framed, spatial, bias, woven):
    shift = jnp.concatenate([bias[...].reshape(1, OUTC), jnp.zeros((1, WIDE - OUTC), F32)], axis=1)
    for parity_row in range(2):
        for parity_col in range(2):
            phase = parity_row * 2 + parity_col
            lanes = slice(parity_col * C, (parity_col + 2) * C)
            result = shift
            for near in range(2):
                rows = slice(parity_row + near, parity_row + near + OWN)
                result = result + dot(
                    framed[:, rows, :, lanes].reshape(2 * OWN * W, 2 * C),
                    spatial[phase, near],
                )
            for frame in range(2):
                for row in range(OWN):
                    start = (frame * OWN + row) * W
                    for lane in range(2):
                        woven[
                            lane, frame, 2 * row + parity_row, pl.ds(parity_col, W, stride=2), :
                        ] = result[start : start + W, lane * 128 : lane * 128 + 128]


def weave_step(woven, out, target, frame0, sems):
    copies = []
    for frame in range(2):
        for row in range(2 * OWN):
            out[frame, row, :, :128] = woven[0, frame, row].astype(BF16)
            out[frame, row, :, 128:] = woven[1, frame, row][:, : OUTC - 128].astype(BF16)
        copies.append(
            pltpu.make_async_copy(out.at[frame], target.at[frame0 + frame], sems.at[frame])
        )
        copies[-1].start()
    return copies


def upsampled(last_col, spatial, bias, target, frame0, first, second):
    frame_step(first[0], last_col, first[1])
    spatial_step(first[1], spatial, bias, first[2])
    frame_step(second[0], last_col, second[1])
    spatial_step(second[1], spatial, bias, second[2])
    copies = weave_step(first[2], first[3], target, frame0, first[4])
    copies += weave_step(second[2], second[3], target, frame0 + 2, second[4])
    for copy in copies:
        copy.wait()


def last_frames_kernel(
    last_col, part, onward, near, mixed, time, time_bias, spatial, spatial_bias, begun, target,
    *scratch,
):
    first_half, second_half = scratch[:5], scratch[5:]
    core = lax.axis_index("row")

    def whole_block(frame):
        own = onward[frame, : OWN * W].astype(F32)
        extra = near[frame].astype(F32)
        rows = jnp.where(
            core == 0,
            jnp.concatenate([own, extra], axis=0),
            jnp.concatenate([extra, own], axis=0),
        )
        return jnp.concatenate([rows, onward[frame, OWN * W :].astype(F32)], axis=0)

    first = (part[0] + whole_block(0)).astype(BF16)
    second = (part[1] + whole_block(1)).astype(BF16)
    whole = time[...].reshape(3 * C, 2 * C)
    shift = time_bias[...].reshape(1, 2 * C)
    first_half[0][...] = (
        dot(jnp.concatenate([first, second, mixed[0]], axis=1), whole) + shift
    )
    second_half[0][...] = (
        dot(jnp.concatenate([second, mixed[0], mixed[1]], axis=1), whole) + shift
    )
    begun[0] = dot(first, whole[2 * C :]) + shift
    begun[1] = dot(jnp.concatenate([first, second], axis=1), whole[C:]) + shift
    upsampled(last_col, spatial, spatial_bias, target, 4, first_half, second_half)


def first_frames_kernel(
    last_col, previous, begun, time, spatial, spatial_bias, half_done, target, *scratch
):
    del half_done
    first_half, second_half = scratch[:5], scratch[5:]
    whole = time[...].reshape(3 * C, 2 * C)
    first_half[0][...] = begun[0] + dot(
        jnp.concatenate([previous[0], previous[1]], axis=1), whole[: 2 * C]
    )
    second_half[0][...] = begun[1] + dot(previous[1], whole[:C])
    upsampled(last_col, spatial, spatial_bias, target, 0, first_half, second_half)


def parity_weights(weight, phases):
    for start, count in ((0, 128), (128, OUTC - 128)):
        part = slice(start, start + count)
        wide = [[weight[row, col, part, :].astype(F32) for col in range(3)] for row in range(3)]
        for parity_row in range(2):
            for near in range(2):
                first, last = ((0, 0), (1, 2)) if parity_row == 0 else ((0, 1), (2, 2))
                low, high = (first, last)[near]
                taps = wide[low]
                if high > low:
                    taps = [one + other for one, other in zip(wide[low], wide[high])]
                for parity_col in range(2):
                    phase = parity_row * 2 + parity_col
                    if parity_col == 0:
                        pair = [taps[0], taps[1] + taps[2]]
                    else:
                        pair = [taps[0] + taps[1], taps[2]]
                    for index in range(2):
                        block = pair[index]
                        if count < 128:
                            none = jnp.zeros((128 - count, C), F32)
                            block = jnp.concatenate([block, none], axis=0)
                        phases[phase, near, index * C : (index + 1) * C, start : start + 128] = (
                            block.T.astype(BF16)
                        )


def cost(macs, bytes_accessed):
    return pl.CostEstimate(flops=2 * macs, bytes_accessed=bytes_accessed, transcendentals=0)


def call(kernel, name, estimate, limit=LIMIT, **rest):
    return pl.pallas_call(
        kernel,
        name=name,
        cost_estimate=estimate,
        compiler_params=pltpu.CompilerParams(vmem_limit_bytes=limit * 2**20),
        **rest,
    )


def swap_rows(block):
    return lax.ppermute(block, "row", [(0, 1), (1, 0)])


def to_later_frames(block):
    return lax.ppermute(block, "tm", [(i, i + 1) for i in range(lax.axis_size("tm") - 1)])


def across_columns(block):
    count = lax.axis_size("col")
    route = [(i, i - 1) for i in range(1, count)]
    route += [(count + i, count + i + 1) for i in range(count - 1)]
    return lax.ppermute(block, ("row", "col"), route)


def on_device(
    latents, norm_gain, conv_weight, conv_bias, time_weight, time_bias, spatial_weight, spatial_bias
):
    last_col = lax.axis_size("col") - 1
    other = swap_rows(latents)
    own = latents
    spatial_weight = jnp.swapaxes(spatial_weight, 2, 3)
    held = call(
        own_edge_kernel,
        "own_edge",
        cost(2**33, 2**20),
        out_shape=jax.ShapeDtypeStruct((8, 8, C), F32),
        in_specs=[VMEM],
        out_specs=VMEM,
    )(own)
    edge = call(
        edge_kernel,
        "edge",
        cost(2**33, 2**20),
        out_shape=jax.ShapeDtypeStruct((4, 2, 8, C), BF16),
        in_specs=[VMEM] * 2,
        out_specs=VMEM,
        scratch_shapes=[pltpu.VMEM((8, 8, C), F32)],
    )(held, other)
    mine = across_columns(edge)

    inner_shape = jax.ShapeDtypeStruct((MROWS * W, 2 * C), F32)
    inner_cost = cost(2 * MROWS * W * 9 * C * C, 7 * 2**20)
    activated, edges, inner3, inner1, inner0, patches2, patches0 = call(
        activate_kernel,
        "activated",
        cost(4 * MROWS * W * 9 * C * C, 7 * 2**20),
        out_shape=(
            jax.ShapeDtypeStruct((4, MROWS + 2, W, C), BF16),
            jax.ShapeDtypeStruct((4, 2, 8, C), F32),
            inner_shape,
            inner_shape,
            jax.ShapeDtypeStruct((MROWS * W, C), F32),
            jax.ShapeDtypeStruct((MROWS * W, 9 * C), BF16),
            jax.ShapeDtypeStruct((MROWS * W, 9 * C), BF16),
        ),
        in_specs=[VMEM] * 4,
        out_specs=(VMEM,) * 7,
        scratch_shapes=2 * [pltpu.VMEM((MROWS * W, 9 * C), BF16)],
    )(own, other, norm_gain, conv_weight)
    mine, activated, patches2 = lax.optimization_barrier((mine, activated, patches2))
    theirs = swap_rows(mine)
    inner2 = call(
        inner_kernel,
        "inner",
        inner_cost,
        out_shape=inner_shape,
        in_specs=[VMEM] * 2,
        out_specs=VMEM,
    )(patches2, conv_weight)

    mixed_shape = jax.ShapeDtypeStruct((2, BLOCK, C), BF16)
    onward, crossing, outer = call(
        send_kernel,
        "partial_for_next",
        cost(2 * 96 * 9 * C * C, 10 * 2**20),
        out_shape=(
            jax.ShapeDtypeStruct((2, SENT, C), BF16),
            jax.ShapeDtypeStruct((2, BLOCK, C), F32),
            jax.ShapeDtypeStruct((4, 4, 8, C), F32),
        ),
        in_specs=[VMEM] * 9,
        out_specs=(VMEM,) * 3,
        scratch_shapes=[pltpu.VMEM((128, 9 * C), BF16), pltpu.VMEM((4, BLOCK, 2 * C), F32)],
    )(edges, mine, theirs, norm_gain, conv_weight, inner0, inner1, inner2, inner3)
    onward = to_later_frames(onward)

    frame_patches = pltpu.VMEM((BLOCK, 9 * C), BF16)
    mixed = call(
        own_kernel,
        "mixed_last",
        cost(3 * BLOCK * 9 * C * C, 10 * 2**20),
        out_shape=mixed_shape,
        in_specs=[VMEM] * 11,
        out_specs=VMEM,
        scratch_shapes=[frame_patches, frame_patches],
    )(
        patches0, activated, edges, outer, conv_weight, crossing, own, other, mine, theirs,
        conv_bias,
    )
    previous = to_later_frames(mixed)

    out_shape = jax.ShapeDtypeStruct((8, 2 * OWN, 2 * W, OUTC), BF16)
    scratch = 2 * [
        pltpu.VMEM((BLOCK, 2 * C), F32),
        pltpu.VMEM((2, OWN + 2, W, 3 * C), BF16),
        pltpu.VMEM((2, 2, 2 * OWN, 2 * W, 128), F32),
        pltpu.VMEM((2, 2 * OWN, 2 * W, OUTC), BF16),
        pltpu.SemaphoreType.DMA((2,)),
    ]
    late_cost = cost(2 * BLOCK * 6 * C * C + 16 * 512 * C * WIDE, 6 * 2**20)

    part, spatial = call(
        first_part_kernel,
        "mixed_first",
        cost(3 * BLOCK * 9 * C * C, 10 * 2**20),
        out_shape=(
            jax.ShapeDtypeStruct((2, BLOCK, C), F32),
            jax.ShapeDtypeStruct((4, 2, 2 * C, WIDE), BF16),
        ),
        in_specs=[VMEM] * 10,
        out_specs=(VMEM,) * 2,
        scratch_shapes=[frame_patches, frame_patches],
    )(
        activated, edges, outer, conv_weight, own, other, mine, theirs, conv_bias,
        spatial_weight,
    )

    onward, part = lax.optimization_barrier((onward, part))
    near = jnp.where(
        lax.axis_index("row") == 0, onward[:, (OWN - 1) * W : OWN * W], onward[:, :W]
    )
    near = swap_rows(near)

    def last_frames(*refs):
        last_frames_kernel(last_col, *refs)

    begun, half_done = call(
        last_frames,
        "upsample_last",
        late_cost,
        out_shape=(jax.ShapeDtypeStruct((2, BLOCK, 2 * C), F32), out_shape),
        in_specs=[VMEM] * 8,
        out_specs=(VMEM, HBM),
        scratch_shapes=scratch,
    )(part, onward, near, mixed, time_weight, time_bias, spatial, spatial_bias)

    def first_frames(*refs):
        first_frames_kernel(last_col, *refs)

    return call(
        first_frames,
        "upsample_first",
        late_cost,
        out_shape=out_shape,
        in_specs=[VMEM] * 5 + [HBM],
        out_specs=HBM,
        scratch_shapes=scratch,
        input_output_aliases={5: 0},
    )(previous, begun, time_weight, spatial, spatial_bias, half_done)


def solution(mesh):
    placed = (P("tm", "row", "col", None), P(), P(), P(), P(), P(), P(), P())
    return jax.shard_map(
        on_device,
        mesh=mesh,
        in_specs=placed,
        out_specs=P("tm", "row", "col", None),
        check_vma=False,
    )
```
